512 devices in a mesh: row: 64 (over y, z), col: 8 (over x, core).
Axes of the slice: x: 4, y: 4, z: 16, core: 2. Of those that a mesh axis runs over, the one named last changes fastest.
Arguments:
- source_points: bfloat16 [8192, 128], P('row'), may hold values from -2.375 to 2.375
- target_points: bfloat16 [131072, 128], P(('col', 'row')), may hold values from -2.375 to 2.375
- source_mass: float32 [64, 128], P('row'), may hold values from 0.5 to 2
- target_mass: float32 [1024, 128], P('col'), may hold values from 0.5 to 2
- tile_list: int32 [64, 8, 2, 16], P('row', 'col'), may hold values from 0 to 127, as said below
- tile_count: int32 [64, 8], P('row', 'col'), may hold values from 1 to 16, as said below
Outputs:
- source_potential: float32 [64, 128], P('row')
- target_potential: float32 [1024, 128], P('col')
The draws below stay inside these ranges and needn't reach their ends.
Inputs may be any that keep to these rules, and one draw needn't show every extreme that they name: `tile_list`: entry 0 is a local source block below 1, entry 1 a local target block below 128; the live slots of a device name distinct pairs; every source block and every target block belongs to some live slot of some device; dead slots hold valid indices. `tile_count`: some device is full in every draw.
All inputs are finite; a program needn't handle non-finite values.
Results may differ from the reference program's by a relative error of at most 0.0003.
Values may be sent and summed in bfloat16 or wider, within the bound.
A program may use at most 64 MiB of HBM per device.

```python
import math
import jax
import jax.numpy as jnp
from jax import lax

DIM = 128
TILE = 128
RB_DEV = 1
CB_DEV = 128
ITERS = 3
TMAX = 16
NS = 8192
NT = 131072
N_ROW = 64
N_COL = 8


def tile_plan(key):
    pair_total = RB_DEV * CB_DEV
    pair_ids = jnp.arange(pair_total, dtype=jnp.int32)
    blk_row = pair_ids // CB_DEV
    blk_col = pair_ids % CB_DEV
    dev_row = jnp.arange(N_ROW, dtype=jnp.int32)[:, None, None]
    dev_col = jnp.arange(N_COL, dtype=jnp.int32)[None, :, None]
    cover_rows = ((blk_row + dev_row) % N_COL == dev_col) & (blk_col == (blk_row * 37 + dev_row) % CB_DEV)
    cover_cols = ((blk_col + 7 * dev_col) % N_ROW == dev_row) & (blk_row == (blk_col // N_ROW + dev_col) % RB_DEV)
    forced = cover_rows | cover_cols
    rand_key, level_key, full_key = jax.random.split(key, 3)
    noise = jax.random.randint(rand_key, (N_ROW, N_COL, pair_total), 0, 2 ** 19, dtype=jnp.int32)
    priority = noise * pair_total + pair_ids + jnp.where(forced, 2 ** 30, 0).astype(jnp.int32)
    chosen = lax.top_k(priority, TMAX)[1].astype(jnp.int32)
    tiles = jnp.stack([chosen // CB_DEV, chosen % CB_DEV], axis=2).astype(jnp.int32)
    needed = jnp.sum(forced.astype(jnp.int32), axis=2)
    level = jax.random.randint(level_key, (N_ROW, N_COL), 0, 4, dtype=jnp.int32)
    base = jnp.right_shift(jnp.full((N_ROW, N_COL), TMAX, jnp.int32), level)
    counts = jnp.maximum(base, needed)
    full_dev = jax.random.randint(full_key, (), 0, N_ROW * N_COL, dtype=jnp.int32)
    flat_ids = jnp.arange(N_ROW * N_COL, dtype=jnp.int32).reshape(N_ROW, N_COL)
    counts = jnp.where(flat_ids == full_dev, TMAX, counts).astype(jnp.int32)
    return (tiles, counts)


def draw_tile_list(key, part):
    tiles, counts = tile_plan(key)
    return tiles


def draw_tile_count(key, part):
    tiles, counts = tile_plan(key)
    return counts


def embed_points(key, point_total):
    points = jnp.clip(0.3 * jax.random.normal(key, (point_total, DIM), jnp.float32), -2.375, 2.375)
    return points


def far_rows(key, points, every):
    sign_key, level_key = jax.random.split(key)
    point_total = points.shape[0]
    signs = jnp.where(jax.random.bernoulli(sign_key, 0.5, (point_total, DIM)), 1.0, -1.0).astype(jnp.float32)
    target_cost = jax.random.uniform(level_key, (point_total, 1), jnp.float32, 96.0, 144.0)
    magnitude = jnp.minimum(2.375, jnp.sqrt(2.0 * target_cost / DIM))
    chosen = (jnp.arange(point_total, dtype=jnp.int32) % every == 5)[:, None]
    return jnp.where(chosen, signs * magnitude, points)


def draw_source_points(key, part):
    key = jax.random.fold_in(key, 11)
    value_key, far_key = jax.random.split(key)
    points = embed_points(value_key, NS)
    return far_rows(far_key, points, 64).astype(jnp.bfloat16)


def draw_target_points(key, part):
    key = jax.random.fold_in(key, 12)
    return embed_points(key, NT).astype(jnp.bfloat16)


def levels(rng, extent, pieces, low, largest):
    def one(position, shards_of):
        steps = jax.random.uniform(jax.random.fold_in(jax.random.fold_in(rng, 6), position), (shards_of,), jnp.float32, low / len(pieces), largest / len(pieces))
        return jnp.repeat(jnp.exp(steps), extent[position] // shards_of).reshape((-1,) + (1,) * (len(extent) - position - 1))

    level = one(*pieces[0])
    for cut in pieces[1:]:
        level = level * one(*cut)
    return level


def setup_inputs(seed: int = 0) -> dict:
    arg_keys = jax.random.split(jax.random.key(seed), 7)
    source_points = draw_source_points(jax.random.fold_in(arg_keys[6], 71), 0)
    target_points = draw_target_points(jax.random.fold_in(arg_keys[6], 71), 0)
    source_mass = jnp.clip(jnp.exp(math.log(2.0) - 1.3862944 * jax.random.uniform(arg_keys[2], (NS // TILE, TILE), jnp.float32) ** levels(arg_keys[2], (NS // TILE, TILE), ((0, 64),), -0.2, 0.2)), 0.5, 2.0)
    target_mass = jnp.clip(jnp.exp(math.log(2.0) - 1.3862944 * jax.random.uniform(arg_keys[3], (NT // TILE, TILE), jnp.float32) ** levels(arg_keys[3], (NT // TILE, TILE), ((0, 8),), -0.2, 0.2)), 0.5, 2.0)
    tile_list = draw_tile_list(jax.random.fold_in(arg_keys[6], 71), 0)
    tile_count = draw_tile_count(jax.random.fold_in(arg_keys[6], 71), 0)
    return dict(source_points=source_points, target_points=target_points, source_mass=source_mass, target_mass=target_mass, tile_list=tile_list, tile_count=tile_count)


EPSILON = 0.5
LOWEST = -1e30


def settle(maxima, totals, block_ids, live_flat, block_total):
    live_col = live_flat[:, None]
    best = jnp.full((block_total, TILE), LOWEST, jnp.float32).at[block_ids].max(jnp.where(live_col, maxima, LOWEST))
    slot_best = best[block_ids]
    weight = jnp.where(live_col, totals * jnp.exp(jnp.where(live_col, maxima, slot_best) - slot_best), 0.0)
    summed = jnp.zeros((block_total, TILE), jnp.float32).at[block_ids].add(weight)
    return best + jnp.log(summed)


def reference(source_points, target_points, source_mass, target_mass, tile_list, tile_count):
    src_blocks = source_points.astype(jnp.float32).reshape(N_ROW * RB_DEV, TILE, DIM)
    dst_blocks = target_points.astype(jnp.float32).reshape(N_COL * CB_DEV, TILE, DIM)
    src_norms = jnp.sum(src_blocks * src_blocks, axis=2)
    dst_norms = jnp.sum(dst_blocks * dst_blocks, axis=2)
    row_base = (jnp.arange(N_ROW, dtype=jnp.int32) * RB_DEV)[:, None, None]
    col_base = (jnp.arange(N_COL, dtype=jnp.int32) * CB_DEV)[None, :, None]
    src_ids = (row_base + tile_list[:, :, 0, :].astype(jnp.int32)).reshape(N_ROW * N_COL, TMAX)
    dst_ids = (col_base + tile_list[:, :, 1, :].astype(jnp.int32)).reshape(N_ROW * N_COL, TMAX)
    live_flat = (jnp.arange(TMAX, dtype=jnp.int32)[None, None, :] < tile_count[:, :, None]).reshape(-1)

    def tile_costs(src_one, dst_one):
        cross = jnp.einsum("tad,tbd->tab", src_blocks[src_one], dst_blocks[dst_one], precision=lax.Precision.HIGHEST)
        return 0.5 * (src_norms[src_one][:, :, None] + dst_norms[dst_one][:, None, :]) - cross

    target_potential = jnp.zeros((N_COL * CB_DEV, TILE), jnp.float32)
    source_potential = jnp.zeros((N_ROW * RB_DEV, TILE), jnp.float32)
    for iteration in range(ITERS):
        def source_side(pair):
            src_one, dst_one = pair
            scores = (target_potential[dst_one][:, None, :] - tile_costs(src_one, dst_one)) / EPSILON
            maxima = jnp.max(scores, axis=2)
            return maxima, jnp.sum(jnp.exp(scores - maxima[:, :, None]), axis=2)

        maxima, totals = lax.map(source_side, (src_ids, dst_ids))
        log_total = settle(maxima.reshape(-1, TILE), totals.reshape(-1, TILE), src_ids.reshape(-1), live_flat, N_ROW * RB_DEV)
        source_potential = EPSILON * (jnp.log(source_mass) - log_total)

        def target_side(pair):
            src_one, dst_one = pair
            scores = (source_potential[src_one][:, :, None] - tile_costs(src_one, dst_one)) / EPSILON
            maxima = jnp.max(scores, axis=1)
            return maxima, jnp.sum(jnp.exp(scores - maxima[:, None, :]), axis=1)

        maxima, totals = lax.map(target_side, (src_ids, dst_ids))
        log_total = settle(maxima.reshape(-1, TILE), totals.reshape(-1, TILE), dst_ids.reshape(-1), live_flat, N_COL * CB_DEV)
        target_potential = EPSILON * (jnp.log(target_mass) - log_total)
    return source_potential, target_potential
```

```python
import functools
import math

import jax
import jax.numpy as jnp
from jax import lax
from jax.experimental import pallas as pl
from jax.experimental.pallas import tpu as pltpu
from jax.sharding import PartitionSpec as P

ITERS = 3
EPSILON = 0.5
LOWEST = -1e30
SCALE = math.log2(math.e) / EPSILON
TILE = 128
OWN = 2
MESH = pl.DeviceIdType.MESH


def far_first(count):
    return sorted(range(1, count), key=lambda d: (-min(d, count - d), d))


def half_norms(points):
    wide = points.astype(jnp.float32)
    square = wide * wide
    high = square.astype(jnp.bfloat16)
    low = (square - high.astype(jnp.float32)).astype(jnp.bfloat16)
    ones = jnp.ones((8, points.shape[1]), jnp.bfloat16)
    total = cross(ones, high) + cross(ones, low)
    return total[0:1] * (0.5 * SCALE)


def cross(left, right):
    return lax.dot_general(
        left, right, (((1,), (1,)), ((), ())), preferred_element_type=jnp.float32
    )


def merge(parts):
    top = jnp.max(parts, axis=0)
    return top + jnp.log2(jnp.sum(jnp.exp2(parts - top[None]), axis=0))


def kernel(
    dims,
    src_ref,
    tgt_ref,
    smass_ref,
    tmass_ref,
    list_ref,
    count_ref,
    osrc_ref,
    otgt_ref,
    full,
    tall,
    meta,
    bias,
    ts_score,
    st_score,
    columns,
    s_top,
    s_sum,
    t_top,
    t_sum,
    lbuf,
    rbuf,
    zbuf,
    qbuf,
    ybuf,
    obuf,
    first_send,
    first_recv,
    iter_send,
    iter_recv,
):
    ny, nz, nx, nk = dims
    owners = nx * nk
    blocks = OWN * ny
    row, col = lax.axis_index("row"), lax.axis_index("col")
    y, z = lax.div(row, nz), lax.rem(row, nz)
    x, k = lax.div(col, nk), lax.rem(col, nk)

    def at_y(d):
        return (lax.rem(y + d, ny) * nz + z, col)

    def at_z(d):
        return (y * nz + lax.rem(z + d, nz), col)

    def at_x(d):
        return (row, lax.rem(x + d, nx) * nk + k)

    def at_k(d):
        return (row, x * nk + lax.rem(k + d, nk))

    def at_col(d):
        return (row, lax.rem(col + d, owners))

    def send(src, dst, sems, where):
        pltpu.make_async_remote_copy(
            src_ref=src,
            dst_ref=dst,
            send_sem=sems[0],
            recv_sem=sems[1],
            device_id=where,
            device_id_type=MESH,
        ).start()

    def settle(ref, sem):
        pltpu.make_async_copy(ref, ref, sem).wait()

    barrier = pltpu.get_barrier_semaphore()
    partners = (
        [at_z(d) for d in far_first(nz)]
        + [at_y(d) for d in far_first(ny)]
        + [at_col(d) for d in far_first(owners)]
    )
    for where in partners:
        pl.semaphore_signal(barrier, inc=1, device_id=where, device_id_type=MESH)

    lane = lax.broadcasted_iota(jnp.int32, (1, TILE), 1)
    count = count_ref[0, 0]
    live = jnp.zeros((1, TILE), jnp.float32)
    for slot in range(list_ref.shape[3]):
        block = jnp.where(slot < count, list_ref[0, 0, 1, slot], -1)
        live = jnp.where(lane == block, 1.0, live)
    meta[z, :, 0:TILE] = jnp.where(live > 0.5, 0.0, LOWEST)
    meta[z, :, TILE : 2 * TILE] = jnp.log2(smass_ref[...])
    part = TILE // owners
    full[z, x, k] = src_ref[pl.ds(pl.multiple_of(col * part, part), part), :]
    tall[y] = tgt_ref[...]

    pl.semaphore_wait(barrier, len(partners))

    def sems(stage):
        return first_send.at[stage], first_recv.at[stage]

    for d in far_first(nz):
        send(meta.at[z], meta.at[z], sems(0), at_z(d))
        send(full.at[z, x, k], full.at[z, x, k], sems(1), at_z(d))
    for d in far_first(ny):
        send(tall.at[y], tall.at[y], sems(2), at_y(d))
    settle(full.at[0 : nz - 1, 0, 0], first_recv.at[1])
    for d in far_first(nx):
        send(full.at[:, x, k], full.at[:, x, k], sems(3), at_x(d))
    if nx > 1:
        settle(full.at[:, 0 : nx - 1, 0], first_recv.at[3])
    for d in far_first(nk):
        send(full.at[:, :, k], full.at[:, :, k], sems(4), at_k(d))

    settle(meta.at[0 : nz - 1], first_recv.at[0])
    drop = meta[:, 0, 0:TILE]
    for tb in range(blocks):
        mine = OWN * nz * (tb // OWN) + OWN * z + tb % OWN
        picked = jnp.sum(jnp.where(lane == mine, drop, 0.0), axis=1, keepdims=True)
        bias[tb] = jnp.broadcast_to(picked, (nz, TILE))
    settle(tall.at[0 : ny - 1], first_recv.at[2])
    half = [
        half_norms(tall[tb // OWN, (tb % OWN) * TILE : (tb % OWN + 1) * TILE, :])
        for tb in range(blocks)
    ]
    tgt_half = jnp.concatenate(half, axis=0)
    src_half = half_norms(src_ref[...])
    src_log = meta[pl.ds(OWN * col, OWN), :, TILE : 2 * TILE]
    tgt_log = jnp.log2(
        jnp.concatenate(
            [tmass_ref[pl.ds(OWN * nz * yy + OWN * z, OWN), :] for yy in range(ny)], axis=0
        )
    )
    if nk > 1:
        settle(full.at[:, :, 0 : nk - 1], first_recv.at[4])

    def build(zz, carry):
        source = full[zz].reshape(TILE, TILE)
        for tb in range(blocks):
            target = tall[tb // OWN, (tb % OWN) * TILE : (tb % OWN + 1) * TILE, :]
            off = bias[tb, pl.ds(zz, 1), :]
            ts_score[zz, tb * TILE : (tb + 1) * TILE, :] = cross(target, source) * SCALE + off
            rows = pl.ds(pl.multiple_of(zz * TILE, TILE), TILE)
            st_score[tb, rows, :] = cross(source, target) * SCALE + off
        return carry

    lax.fori_loop(0, nz, build, 0)

    def stand(rows):
        turned = jnp.transpose(rows)
        for b in range(rows.shape[0]):
            columns[b * TILE : (b + 1) * TILE, :] = jnp.broadcast_to(
                turned[:, b : b + 1], (TILE, TILE)
            )

    def reduce(score, tops, sums, outer, inner):
        def step(b, carry):
            for i in range(inner):
                at = slice(i * TILE, (i + 1) * TILE)
                s = (score[b, at, :] + columns[at, :]).reshape(TILE // 8, 8, TILE)
                top = jnp.max(s, axis=0)
                tops[b, i * 8 : (i + 1) * 8, :] = top
                sums[b, i * 8 : (i + 1) * 8, :] = jnp.sum(jnp.exp2(s - top[None]), axis=0)
            return carry

        lax.fori_loop(0, outer, step, 0)
        top = jnp.max(tops[...], axis=1)
        total = jnp.sum(jnp.exp2(tops[...] - top[:, None, :]) * sums[...], axis=1)
        return top + jnp.log2(total)

    def pair(it, stage):
        return iter_send.at[it, stage], iter_recv.at[it, stage]

    tgt_pot = -tgt_half
    for it in range(ITERS):
        stand(tgt_pot)
        part_sum = reduce(ts_score, s_top, s_sum, nz, blocks)
        for b in range(nz):
            lbuf[it, b] = part_sum[b : b + 1, :]
        for d in far_first(owners):
            other = lax.rem(col + d, owners)
            send(
                lbuf.at[it, pl.ds(OWN * other, OWN)], rbuf.at[it, col], pair(it, 0), at_col(d)
            )
        rbuf[it, col] = lbuf[it, pl.ds(OWN * col, OWN)]
        settle(rbuf.at[it, 0 : owners - 1], iter_recv.at[it, 0])
        zbuf[it, z] = merge(rbuf[it])
        for d in far_first(nz):
            send(zbuf.at[it, z], zbuf.at[it, z], pair(it, 1), at_z(d))
        settle(zbuf.at[it, 0 : nz - 1], iter_recv.at[it, 1])
        qbuf[it, pl.ds(OWN * col, OWN)] = src_log - merge(zbuf[it])
        for d in far_first(owners):
            mine = qbuf.at[it, pl.ds(OWN * col, OWN)]
            send(mine, mine, pair(it, 2), at_col(d))
        settle(qbuf.at[it, 0 : nz - OWN], iter_recv.at[it, 2])
        stand(qbuf[it, :, 0, :])
        ybuf[it, y] = reduce(st_score, t_top, t_sum, blocks, nz)
        for d in far_first(ny):
            send(ybuf.at[it, y], ybuf.at[it, y], pair(it, 3), at_y(d))
        settle(ybuf.at[it, 0 : ny - 1], iter_recv.at[it, 3])
        tgt_pot = tgt_log - merge(ybuf[it])

    obuf[z] = (tgt_pot + tgt_half) * (1.0 / SCALE)
    for d in far_first(nz):
        send(obuf.at[z], obuf.at[z], sems(5), at_z(d))
    osrc_ref[...] = (qbuf[ITERS - 1, z] + src_half) * (1.0 / SCALE)

    settle(meta.at[0 : nz - 1], first_send.at[0])
    settle(full.at[0 : nz - 1, 0, 0], first_send.at[1])
    settle(tall.at[0 : ny - 1], first_send.at[2])
    if nx > 1:
        settle(full.at[:, 0 : nx - 1, 0], first_send.at[3])
    if nk > 1:
        settle(full.at[:, :, 0 : nk - 1], first_send.at[4])
    for it in range(ITERS):
        settle(rbuf.at[it, 0 : owners - 1], iter_send.at[it, 0])
        settle(zbuf.at[it, 0 : nz - 1], iter_send.at[it, 1])
        settle(qbuf.at[it, 0 : nz - OWN], iter_send.at[it, 2])
        settle(ybuf.at[it, 0 : ny - 1], iter_send.at[it, 3])
    settle(obuf.at[0 : nz - 1], first_recv.at[5])
    settle(obuf.at[0 : nz - 1], first_send.at[5])
    for zz in range(nz):
        for yy in range(ny):
            at = OWN * (yy * nz + zz)
            otgt_ref[at : at + OWN, :] = obuf[zz, OWN * yy : OWN * (yy + 1), :]


def body(dims, *args):
    ny, nz, nx, nk = dims
    owners = nx * nk
    blocks = OWN * ny
    vmem = pl.BlockSpec(memory_space=pltpu.VMEM)
    smem = pl.BlockSpec(memory_space=pltpu.SMEM)
    f32 = jnp.float32
    return pl.pallas_call(
        functools.partial(kernel, dims),
        out_shape=(
            jax.ShapeDtypeStruct((1, TILE), f32),
            jax.ShapeDtypeStruct((blocks * nz, TILE), f32),
        ),
        in_specs=[vmem, vmem, vmem, vmem, smem, smem],
        out_specs=(vmem, vmem),
        scratch_shapes=[
            pltpu.VMEM((nz, nx, nk, TILE // owners, TILE), jnp.bfloat16),
            pltpu.VMEM((ny, OWN * TILE, TILE), jnp.bfloat16),
            pltpu.VMEM((nz, 1, 2 * TILE), f32),
            pltpu.VMEM((blocks, nz, TILE), f32),
            pltpu.VMEM((nz, blocks * TILE, TILE), f32),
            pltpu.VMEM((blocks, nz * TILE, TILE), f32),
            pltpu.VMEM((max(nz, blocks) * TILE, TILE), f32),
            pltpu.VMEM((nz, blocks * 8, TILE), f32),
            pltpu.VMEM((nz, blocks * 8, TILE), f32),
            pltpu.VMEM((blocks, nz * 8, TILE), f32),
            pltpu.VMEM((blocks, nz * 8, TILE), f32),
            pltpu.VMEM((ITERS, nz, 1, TILE), f32),
            pltpu.VMEM((ITERS, owners, OWN, 1, TILE), f32),
            pltpu.VMEM((ITERS, nz, OWN, 1, TILE), f32),
            pltpu.VMEM((ITERS, nz, 1, TILE), f32),
            pltpu.VMEM((ITERS, ny, blocks, TILE), f32),
            pltpu.VMEM((nz, blocks, TILE), f32),
            pltpu.SemaphoreType.DMA((6,)),
            pltpu.SemaphoreType.DMA((6,)),
            pltpu.SemaphoreType.DMA((ITERS, 4)),
            pltpu.SemaphoreType.DMA((ITERS, 4)),
        ],
        compiler_params=pltpu.CompilerParams(
            collective_id=0, has_side_effects=True, vmem_limit_bytes=40 * 2**20
        ),
    )(*args)


def solution(mesh, dims=(4, 16, 4, 2)):
    in_specs = (
        P("row", None),
        P(("col", "row"), None),
        P("row", None),
        P("col", None),
        P("row", "col", None, None),
        P("row", "col"),
    )
    out_specs = (P("row", None), P("col", None))
    return jax.shard_map(
        functools.partial(body, dims),
        mesh=mesh,
        in_specs=in_specs,
        out_specs=out_specs,
        check_vma=False,
    )
```

```python
import functools
import math

import jax
import jax.numpy as jnp
from jax import lax
from jax.experimental import pallas as pl
from jax.experimental.pallas import tpu as pltpu
from jax.sharding import PartitionSpec as P

ITERS = 3
EPSILON = 0.5
LOWEST = -1e30
SCALE = math.log2(math.e) / EPSILON
TILE = 128
OWN = 2
MESH = pl.DeviceIdType.MESH


def far_first(count):
    return sorted(range(1, count), key=lambda d: (-min(d, count - d), d))


def cross(left, right):
    return lax.dot_general(
        left, right, (((1,), (1,)), ((), ())), preferred_element_type=jnp.float32
    )


def half_norms(points):
    wide = points.astype(jnp.float32)
    square = wide * wide
    high = square.astype(jnp.bfloat16)
    low = (square - high.astype(jnp.float32)).astype(jnp.bfloat16)
    ones = jnp.ones((8, points.shape[1]), jnp.bfloat16)
    total = cross(ones, high) + cross(ones, low)
    return total[0:1] * (0.5 * SCALE)


def merge(parts):
    top = jnp.max(parts, axis=0)
    return top + jnp.log2(jnp.sum(jnp.exp2(parts - top[None]), axis=0))


def fold(s):
    s = s.reshape(s.shape[0] // 8, 8, TILE)
    top = jnp.max(s, axis=0)
    return top, jnp.sum(jnp.exp2(s - top[None]), axis=0)


def close(tops, sums):
    top = jnp.max(tops, axis=1)
    total = jnp.sum(jnp.exp2(tops - top[:, None, :]) * sums, axis=1)
    return top + jnp.log2(total)


def kernel(
    dims,
    src_hbm,
    tgt_hbm,
    smass_hbm,
    tmass_hbm,
    list_hbm,
    count_hbm,
    osrc_ref,
    otgt_ref,
    src,
    tmass,
    smass,
    slots,
    count,
    full,
    tall,
    own,
    meta,
    hold,
    logs,
    bias,
    ts_score,
    st_score,
    columns,
    s_top,
    s_sum,
    t_top,
    t_sum,
    xbuf,
    zbuf,
    ybuf,
    qrow,
    sib,
    pots,
    obuf,
    local_sem,
    piece_sem,
    first_send,
    first_recv,
    iter_send,
    iter_recv,
):
    ny, nz, nx, nk = dims
    group = ny * nk
    held = nz // nk
    blocks = OWN * group
    part = TILE // nx
    row, col = lax.axis_index("row"), lax.axis_index("col")
    y, z = lax.div(row, nz), lax.rem(row, nz)
    x, k = lax.div(col, nk), lax.rem(col, nk)
    seat = y * nk + k
    mine = lax.div(z, nk)
    shift = lax.rem(k + nz - lax.rem(z, nk), nk)

    def at_z(d):
        return (y * nz + lax.rem(z + d, nz), col)

    def at_x(d):
        return (row, lax.rem(x + d, nx) * nk + k)

    def at_k(d):
        return (row, x * nk + lax.rem(k + d, nk))

    def at_seat(d):
        other = lax.rem(seat + d, group)
        return (lax.div(other, nk) * nz + z, x * nk + lax.rem(other, nk))

    def send(src_ref, dst_ref, sems, where):
        pltpu.make_async_remote_copy(
            src_ref=src_ref,
            dst_ref=dst_ref,
            send_sem=sems[0],
            recv_sem=sems[1],
            device_id=where,
            device_id_type=MESH,
        ).start()

    def settle(ref, sem):
        pltpu.make_async_copy(ref, ref, sem).wait()

    loads = [
        pltpu.make_async_copy(src_hbm, src, local_sem.at[0]),
        pltpu.make_async_copy(tgt_hbm, tall.at[seat], local_sem.at[1]),
        pltpu.make_async_copy(smass_hbm, smass, local_sem.at[2]),
        pltpu.make_async_copy(tmass_hbm, tmass, local_sem.at[3]),
        pltpu.make_async_copy(list_hbm, slots, local_sem.at[4]),
        pltpu.make_async_copy(count_hbm, count, local_sem.at[5]),
    ]
    for load in loads:
        load.start()

    barrier = pltpu.get_barrier_semaphore()
    partners = (
        [at_z(d) for d in far_first(nz)]
        + [at_seat(d) for d in range(1, group)]
        + [at_x(d) for d in far_first(nx)]
    )
    for where in partners:
        pl.semaphore_signal(barrier, inc=1, device_id=where, device_id_type=MESH)
    for load in loads:
        load.wait()

    lane = lax.broadcasted_iota(jnp.int32, (1, TILE), 1)
    used = count[0, 0]
    live = jnp.zeros((1, TILE), jnp.float32)
    for slot in range(slots.shape[3]):
        block = jnp.where(slot < used, slots[0, 0, 1, slot], -1)
        live = jnp.where(lane == block, 1.0, live)
    own[0, :, 0:TILE] = jnp.where(live > 0.5, 0.0, LOWEST)
    own[0, :, TILE : 2 * TILE] = jnp.log2(smass[...])
    for yy in range(ny):
        at = OWN * nz * yy + OWN * z
        logs[yy, k] = jnp.log2(tmass[pl.ds(at, OWN), :])

    pl.semaphore_wait(barrier, len(partners))

    def sems(stage):
        return first_send.at[stage], first_recv.at[stage]

    my_slot = full.at[mine * nx + x]
    my_part = src.at[pl.ds(pl.multiple_of(x * part, part), part)]

    @pl.when(shift == 0)
    def _():
        for d in far_first(nz):
            send(my_part, my_slot, (first_send.at[0], piece_sem.at[0, mine]), at_z(d))
        pltpu.make_async_copy(my_part, my_slot, piece_sem.at[0, mine]).start()

    @pl.when(shift != 0)
    def _():
        send(own.at[0], meta.at[mine, k], sems(1), at_k(1))

    for d in range(1, group):
        send(tall.at[seat], tall.at[seat], sems(3), at_seat(d))
    send(logs.at[:, k], logs.at[:, k], sems(4), at_k(1))

    @pl.when(shift == 0)
    def _():
        meta[mine, k] = own[0]
        settle(own.at[0], first_recv.at[1])
        for d in far_first(nz):
            send(meta.at[mine], meta.at[mine], sems(2), at_z(d))

    def slot_at(i):
        odd = lax.rem(i, 2)
        m = odd * lax.div(i + 1, 2) + (1 - odd) * lax.rem(held - lax.div(i, 2), held)
        return lax.div(lax.rem(z + shift + nk * m, nz), nk)

    def forward(i, carry):
        j = slot_at(i)
        settle(full.at[j * nx + x], piece_sem.at[0, j])
        for d in far_first(nx):
            piece = full.at[j * nx + x]
            send(piece, piece, (first_send.at[5], piece_sem.at[1, j]), at_x(d))
        return carry

    lax.fori_loop(0, held, forward, 0)

    def targets(tb):
        at = tb % OWN * TILE
        return tall[tb // OWN, at : at + TILE, :]

    settle(tall.at[0 : group - 1], first_recv.at[3])
    tgt_half = jnp.concatenate([half_norms(targets(tb)) for tb in range(blocks)], axis=0)
    src_half = half_norms(src[...])

    @pl.when(shift == 0)
    def _():
        settle(meta.at[0 : held - 1], first_recv.at[2])

    @pl.when(shift != 0)
    def _():
        settle(meta, first_recv.at[2])

    for tb in range(blocks):
        drop = meta[:, tb // OWN % nk, 0, 0:TILE]
        at = OWN * nz * (tb // OWN // nk) + OWN * z + tb % OWN
        picked = jnp.sum(jnp.where(lane == at, drop, 0.0), axis=1, keepdims=True)
        bias[tb] = jnp.broadcast_to(picked, (held, TILE))
    src_log = meta[:, 0, 0, TILE : 2 * TILE]
    settle(logs.at[:, 0], first_recv.at[4])
    tgt_log = jnp.concatenate(
        [logs[i // nk, i % nk] for i in range(group)], axis=0
    )

    def stand(rows):
        turned = jnp.transpose(rows)
        for b in range(rows.shape[0]):
            columns[b * TILE : (b + 1) * TILE, :] = jnp.broadcast_to(
                turned[:, b : b + 1], (TILE, TILE)
            )

    def first_half(i, carry):
        j = slot_at(i)
        if nx > 1:
            settle(full.at[pl.ds(j * nx, nx - 1)], piece_sem.at[1, j])
        source = full[pl.ds(j * nx, nx)].reshape(TILE, TILE)
        for tb in range(blocks):
            at = slice(tb * TILE, (tb + 1) * TILE)
            tile = cross(targets(tb), source) * SCALE + bias[tb, pl.ds(j, 1), :]
            ts_score[j, at, :] = tile
            top, total = fold(tile + columns[at, :])
            s_top[j, tb * 8 : (tb + 1) * 8, :] = top
            s_sum[j, tb * 8 : (tb + 1) * 8, :] = total
        return carry

    def source_half(j, carry):
        for tb in range(blocks):
            at = slice(tb * TILE, (tb + 1) * TILE)
            top, total = fold(ts_score[j, at, :] + columns[at, :])
            s_top[j, tb * 8 : (tb + 1) * 8, :] = top
            s_sum[j, tb * 8 : (tb + 1) * 8, :] = total
        return carry

    def build(j, carry):
        source = full[pl.ds(j * nx, nx)].reshape(TILE, TILE)
        rows = pl.ds(pl.multiple_of(j * TILE, TILE), TILE)
        for tb in range(blocks):
            st_score[tb, rows, :] = cross(source, targets(tb)) * SCALE + bias[tb, pl.ds(j, 1), :]
        return carry

    def target_half(tb, carry):
        for j in range(held):
            at = slice(j * TILE, (j + 1) * TILE)
            top, total = fold(st_score[tb, at, :] + columns[at, :])
            t_top[tb, j * 8 : (j + 1) * 8, :] = top
            t_sum[tb, j * 8 : (j + 1) * 8, :] = total
        return carry

    def pair(it, stage):
        return iter_send.at[it, stage], iter_recv.at[it, stage]

    tgt_pot = -tgt_half
    for it in range(ITERS):
        stand(tgt_pot)
        lax.fori_loop(0, held, source_half if it else first_half, 0)
        xbuf[it, x] = close(s_top[...], s_sum[...])
        for d in far_first(nx):
            send(xbuf.at[it, x], xbuf.at[it, x], pair(it, 0), at_x(d))
        if nx > 1:
            settle(xbuf.at[it, 0 : nx - 1], iter_recv.at[it, 0])
        zbuf[it, z] = merge(xbuf[it])
        for d in far_first(nz):
            send(zbuf.at[it, z], zbuf.at[it, z], pair(it, 1), at_z(d))
        if it == 0:
            lax.fori_loop(0, held, build, 0)
        settle(zbuf.at[it, 0 : nz - 1], iter_recv.at[it, 1])
        src_pot = src_log - merge(zbuf[it])
        stand(src_pot)
        if it == ITERS - 1:
            for j in range(held):
                qrow[j] = src_pot[j : j + 1, :]

            @pl.when(shift == 0)
            def _():
                sib[0] = qrow[mine]
                send(sib.at[0], sib.at[1], sems(6), at_k(1))

        lax.fori_loop(0, blocks, target_half, 0)
        ybuf[it, seat] = close(t_top[...], t_sum[...])
        for d in range(1, group):
            send(ybuf.at[it, seat], ybuf.at[it, seat], pair(it, 2), at_seat(d))
        settle(ybuf.at[it, 0 : group - 1], iter_recv.at[it, 2])
        tgt_pot = tgt_log - merge(ybuf[it])

    result = (tgt_pot + tgt_half) * (1.0 / SCALE)
    for i in range(group):
        pots[i] = result[OWN * i : OWN * (i + 1), :]
    for yy in range(ny):
        obuf[z, yy] = pots[yy * nk + k]
    for d in far_first(nz):
        send(obuf.at[z], obuf.at[z], sems(7), at_z(d))

    @pl.when(shift == 0)
    def _():
        osrc_ref[...] = (sib[0] + src_half) * (1.0 / SCALE)
        settle(sib.at[0], first_send.at[6])
        settle(full.at[0 : nz - 1], first_send.at[0])
        settle(hold, first_send.at[2])

    @pl.when(shift != 0)
    def _():
        settle(sib.at[1], first_recv.at[6])
        osrc_ref[...] = (sib[1] + src_half) * (1.0 / SCALE)
        settle(own.at[0], first_send.at[1])

    settle(tall.at[0 : group - 1], first_send.at[3])
    settle(logs.at[:, 0], first_send.at[4])
    if nx > 1:
        settle(full.at[0 : held * (nx - 1)], first_send.at[5])
    for it in range(ITERS):
        if nx > 1:
            settle(xbuf.at[it, 0 : nx - 1], iter_send.at[it, 0])
        settle(zbuf.at[it, 0 : nz - 1], iter_send.at[it, 1])
        settle(ybuf.at[it, 0 : group - 1], iter_send.at[it, 2])
    settle(obuf.at[0 : nz - 1], first_recv.at[7])
    settle(obuf.at[0 : nz - 1], first_send.at[7])
    for zz in range(nz):
        for yy in range(ny):
            at = OWN * (yy * nz + zz)
            otgt_ref[at : at + OWN, :] = obuf[zz, yy]


def body(dims, *args):
    ny, nz, nx, nk = dims
    group = ny * nk
    held = nz // nk
    blocks = OWN * group
    f32, bf16 = jnp.float32, jnp.bfloat16
    dma = pltpu.SemaphoreType.DMA
    return pl.pallas_call(
        functools.partial(kernel, dims),
        out_shape=(
            jax.ShapeDtypeStruct((1, TILE), f32),
            jax.ShapeDtypeStruct((OWN * ny * nz, TILE), f32),
        ),
        in_specs=[pl.BlockSpec(memory_space=pl.ANY)] * 6,
        out_specs=(pl.BlockSpec(memory_space=pltpu.VMEM),) * 2,
        scratch_shapes=[
            pltpu.VMEM(args[0].shape, bf16),
            pltpu.VMEM(args[3].shape, f32),
            pltpu.VMEM(args[2].shape, f32),
            pltpu.SMEM(args[4].shape, jnp.int32),
            pltpu.SMEM(args[5].shape, jnp.int32),
            pltpu.VMEM((held * nx, TILE // nx, TILE), bf16),
            pltpu.VMEM((group, OWN * TILE, TILE), bf16),
            pltpu.VMEM((1, 1, 2 * TILE), f32),
            pltpu.VMEM((held, nk, 1, 2 * TILE), f32),
            pltpu.VMEM((nz - 1, nk, 1, 2 * TILE), f32),
            pltpu.VMEM((ny, nk, OWN, TILE), f32),
            pltpu.VMEM((blocks, held, TILE), f32),
            pltpu.VMEM((held, blocks * TILE, TILE), f32),
            pltpu.VMEM((blocks, held * TILE, TILE), f32),
            pltpu.VMEM((max(held, blocks) * TILE, TILE), f32),
            pltpu.VMEM((held, blocks * 8, TILE), f32),
            pltpu.VMEM((held, blocks * 8, TILE), f32),
            pltpu.VMEM((blocks, held * 8, TILE), f32),
            pltpu.VMEM((blocks, held * 8, TILE), f32),
            pltpu.VMEM((ITERS, nx, held, TILE), f32),
            pltpu.VMEM((ITERS, nz, held, TILE), f32),
            pltpu.VMEM((ITERS, group, blocks, TILE), f32),
            pltpu.VMEM((held, 1, TILE), f32),
            pltpu.VMEM((2, 1, TILE), f32),
            pltpu.VMEM((group, OWN, TILE), f32),
            pltpu.VMEM((nz, ny, OWN, TILE), f32),
            dma((6,)),
            dma((2, held)),
            dma((8,)),
            dma((8,)),
            dma((ITERS, 3)),
            dma((ITERS, 3)),
        ],
        compiler_params=pltpu.CompilerParams(
            collective_id=0, has_side_effects=True, vmem_limit_bytes=56 * 2**20
        ),
    )(*args)


def solution(mesh, dims=(4, 16, 4, 2)):
    in_specs = (
        P("row", None),
        P(("col", "row"), None),
        P("row", None),
        P("col", None),
        P("row", "col", None, None),
        P("row", "col"),
    )
    out_specs = (P("row", None), P("col", None))
    return jax.shard_map(
        functools.partial(body, dims),
        mesh=mesh,
        in_specs=in_specs,
        out_specs=out_specs,
        check_vma=False,
    )
```

```python
import functools
import math

import jax
import jax.numpy as jnp
from jax import lax
from jax.experimental import pallas as pl
from jax.experimental.pallas import tpu as pltpu
from jax.sharding import PartitionSpec as P

ITERS = 3
EPSILON = 0.5
LOWEST = -1e30
SCALE = math.log2(math.e) / EPSILON
TILE = 128
OWN = 2
MESH = pl.DeviceIdType.MESH


def far_first(count):
    return sorted(range(1, count), key=lambda d: (-min(d, count - d), d))


def cross(left, right):
    return lax.dot_general(
        left, right, (((1,), (1,)), ((), ())), preferred_element_type=jnp.float32
    )


def half_norms(points):
    wide = points.astype(jnp.float32)
    square = wide * wide
    high = square.astype(jnp.bfloat16)
    low = (square - high.astype(jnp.float32)).astype(jnp.bfloat16)
    ones = jnp.ones((8, points.shape[1]), jnp.bfloat16)
    total = cross(ones, high) + cross(ones, low)
    return total[0:1] * (0.5 * SCALE)


def merge(parts):
    top = jnp.max(parts, axis=0)
    return top + jnp.log2(jnp.sum(jnp.exp2(parts - top[None]), axis=0))


def fold(s):
    s = s.reshape(s.shape[0] // 8, 8, TILE)
    top = jnp.max(s, axis=0)
    return top, jnp.sum(jnp.exp2(s - top[None]), axis=0)


def close(tops, sums):
    top = jnp.max(tops, axis=1)
    total = jnp.sum(jnp.exp2(tops - top[:, None, :]) * sums, axis=1)
    return top + jnp.log2(total)


def kernel(
    dims,
    src_hbm,
    tgt_hbm,
    smass_hbm,
    tmass_hbm,
    list_hbm,
    count_hbm,
    osrc_ref,
    otgt_ref,
    src,
    tmass,
    smass,
    slots,
    count,
    full,
    tall,
    own,
    meta,
    hold,
    logs,
    halves,
    picks_src,
    picks_tgt,
    bias,
    ts_score,
    st_score,
    columns,
    s_top,
    s_sum,
    t_top,
    t_sum,
    xbuf,
    zbuf,
    ybuf,
    qrow,
    sib,
    pots,
    obuf,
    local_sem,
    piece_sem,
    first_send,
    first_recv,
    iter_send,
    iter_recv,
):
    ny, nz, nx, nk = dims
    group = ny * nk
    held = nz // nk
    blocks = OWN * group
    part = TILE // nx
    row, col = lax.axis_index("row"), lax.axis_index("col")
    y, z = lax.div(row, nz), lax.rem(row, nz)
    x, k = lax.div(col, nk), lax.rem(col, nk)
    seat = y * nk + k
    mine = lax.div(z, nk)
    shift = lax.rem(k + nz - lax.rem(z, nk), nk)

    def at_z(d):
        return (y * nz + lax.rem(z + d, nz), col)

    def at_x(d):
        return (row, lax.rem(x + d, nx) * nk + k)

    def at_k(d):
        return (row, x * nk + lax.rem(k + d, nk))

    def at_seat(d):
        other = lax.rem(seat + d, group)
        return (lax.div(other, nk) * nz + z, x * nk + lax.rem(other, nk))

    def send(src_ref, dst_ref, sems, where):
        pltpu.make_async_remote_copy(
            src_ref=src_ref,
            dst_ref=dst_ref,
            send_sem=sems[0],
            recv_sem=sems[1],
            device_id=where,
            device_id_type=MESH,
        ).start()

    def settle(ref, sem):
        pltpu.make_async_copy(ref, ref, sem).wait()

    loads = [
        pltpu.make_async_copy(src_hbm, src, local_sem.at[0]),
        pltpu.make_async_copy(tgt_hbm, tall.at[seat], local_sem.at[1]),
        pltpu.make_async_copy(smass_hbm, smass, local_sem.at[2]),
        pltpu.make_async_copy(tmass_hbm, tmass, local_sem.at[3]),
        pltpu.make_async_copy(list_hbm, slots, local_sem.at[4]),
        pltpu.make_async_copy(count_hbm, count, local_sem.at[5]),
    ]
    for load in loads:
        load.start()

    barrier = pltpu.get_barrier_semaphore()
    partners = (
        [at_z(d) for d in far_first(nz)]
        + [at_seat(d) for d in range(1, group)]
        + [at_x(d) for d in far_first(nx)]
    )
    for where in partners:
        pl.semaphore_signal(barrier, inc=1, device_id=where, device_id_type=MESH)
    for load in loads:
        load.wait()

    for picks in (picks_src, picks_tgt):
        n = picks.shape[0] // 3
        which = lax.rem(lax.broadcasted_iota(jnp.int32, picks.shape, 0), n)
        place = lax.div(lax.broadcasted_iota(jnp.int32, picks.shape, 1), TILE)
        picks[...] = jnp.where(which == place, 1.0, 0.0).astype(jnp.bfloat16)
    own_half = half_norms(tall[seat])
    for i in range(OWN):
        halves[seat, i : i + 1, :] = own_half[:, i * TILE : (i + 1) * TILE]
    src_half = half_norms(src[...])
    lane = lax.broadcasted_iota(jnp.int32, (1, TILE), 1)
    used = count[0, 0]
    live = jnp.zeros((1, TILE), jnp.float32)
    for slot in range(slots.shape[3]):
        block = jnp.where(slot < used, slots[0, 0, 1, slot], -1)
        live = jnp.where(lane == block, 1.0, live)
    own[0, :, 0:TILE] = jnp.where(live > 0.5, 0.0, LOWEST)
    own[0, :, TILE : 2 * TILE] = jnp.log2(smass[...])
    for yy in range(ny):
        at = OWN * nz * yy + OWN * z
        logs[yy, k] = jnp.log2(tmass[pl.ds(at, OWN), :])

    pl.semaphore_wait(barrier, len(partners))

    def sems(stage):
        return first_send.at[stage], first_recv.at[stage]

    my_slot = full.at[mine * nx + x]
    my_part = src.at[pl.ds(pl.multiple_of(x * part, part), part)]

    @pl.when(shift == 0)
    def _():
        for d in far_first(nz):
            send(my_part, my_slot, (first_send.at[0], piece_sem.at[0, mine]), at_z(d))
        pltpu.make_async_copy(my_part, my_slot, piece_sem.at[0, mine]).start()

    @pl.when(shift != 0)
    def _():
        send(own.at[0], meta.at[mine, k], sems(1), at_k(1))

    for d in range(1, group):
        send(halves.at[seat], halves.at[seat], sems(8), at_seat(d))
    for d in range(1, group):
        send(tall.at[seat], tall.at[seat], sems(3), at_seat(d))
    send(logs.at[:, k], logs.at[:, k], sems(4), at_k(1))

    @pl.when(shift == 0)
    def _():
        meta[mine, k] = own[0]
        settle(own.at[0], first_recv.at[1])
        for d in far_first(nz):
            send(meta.at[mine], meta.at[mine], sems(2), at_z(d))

    def slot_at(i):
        odd = lax.rem(i, 2)
        m = odd * lax.div(i + 1, 2) + (1 - odd) * lax.rem(held - lax.div(i, 2), held)
        return lax.div(lax.rem(z + shift + nk * m, nz), nk)

    def forward(i, carry):
        j = slot_at(i)
        settle(full.at[j * nx + x], piece_sem.at[0, j])
        for d in far_first(nx):
            piece = full.at[j * nx + x]
            send(piece, piece, (first_send.at[5], piece_sem.at[1, j]), at_x(d))
        return carry

    near = max(held - 3, 0)
    lax.fori_loop(0, near, forward, 0)

    @pl.when(shift == 0)
    def _():
        settle(meta.at[0 : held - 1], first_recv.at[2])

    @pl.when(shift != 0)
    def _():
        settle(meta, first_recv.at[2])

    for tb in range(blocks):
        drop = meta[:, tb // OWN % nk, 0, 0:TILE]
        at = OWN * nz * (tb // OWN // nk) + OWN * z + tb % OWN
        picked = jnp.sum(jnp.where(lane == at, drop, 0.0), axis=1, keepdims=True)
        bias[tb] = jnp.broadcast_to(picked, (held, TILE))
    src_log = meta[:, 0, 0, TILE : 2 * TILE]
    settle(logs.at[:, 0], first_recv.at[4])
    tgt_log = jnp.concatenate(
        [logs[i // nk, i % nk] for i in range(group)], axis=0
    )

    def stand(rows):
        n = rows.shape[0]
        high = rows.astype(jnp.bfloat16).astype(jnp.float32)
        rest = rows - high
        middle = rest.astype(jnp.bfloat16).astype(jnp.float32)
        pieces = jnp.concatenate([high, middle, rest - middle], axis=0)
        turned = jnp.transpose(pieces).astype(jnp.bfloat16)
        picks = picks_src if n == held else picks_tgt
        spread = jnp.dot(turned, picks[...], preferred_element_type=jnp.float32)
        for b in range(n):
            columns[b * TILE : (b + 1) * TILE, :] = spread[:, b * TILE : (b + 1) * TILE]

    def first_half(i, carry):
        pair_of = [slot_at(2 * i), slot_at(2 * i + 1)]
        if nx > 1:
            for j in pair_of:
                settle(full.at[pl.ds(j * nx, nx - 1)], piece_sem.at[1, j])
        source = jnp.concatenate(
            [full[pl.ds(j * nx, nx)].reshape(TILE, TILE) for j in pair_of], axis=0
        )
        for g in range(group):
            product = cross(tall[g], source) * SCALE
            for n in range(2 * OWN):
                u, v = n // 2, n % 2
                tb, j = OWN * g + u, pair_of[v]
                at = slice(tb * TILE, (tb + 1) * TILE)
                tile = product[u * TILE : (u + 1) * TILE, v * TILE : (v + 1) * TILE]
                tile = tile + bias[tb, pl.ds(j, 1), :]
                ts_score[j, at, :] = tile
                top, total = fold(tile + columns[at, :])
                s_top[j, tb * 8 : (tb + 1) * 8, :] = top
                s_sum[j, tb * 8 : (tb + 1) * 8, :] = total
        return carry

    def source_half(j, carry):
        for tb in range(blocks):
            at = slice(tb * TILE, (tb + 1) * TILE)
            top, total = fold(ts_score[j, at, :] + columns[at, :])
            s_top[j, tb * 8 : (tb + 1) * 8, :] = top
            s_sum[j, tb * 8 : (tb + 1) * 8, :] = total
        return carry

    def build(j, carry):
        source = full[pl.ds(j * nx, nx)].reshape(TILE, TILE)
        rows = pl.ds(pl.multiple_of(j * TILE, TILE), TILE)
        for g in range(group):
            product = cross(source, tall[g]) * SCALE
            for u in range(OWN):
                tb = OWN * g + u
                tile = product[:, u * TILE : (u + 1) * TILE]
                st_score[tb, rows, :] = tile + bias[tb, pl.ds(j, 1), :]
        return carry

    def target_half(tb, carry):
        for j in range(held):
            at = slice(j * TILE, (j + 1) * TILE)
            top, total = fold(st_score[tb, at, :] + columns[at, :])
            t_top[tb, j * 8 : (j + 1) * 8, :] = top
            t_sum[tb, j * 8 : (j + 1) * 8, :] = total
        return carry

    def pair(it, stage):
        return iter_send.at[it, stage], iter_recv.at[it, stage]

    settle(halves.at[0 : group - 1], first_recv.at[8])
    tgt_half = jnp.concatenate([halves[i] for i in range(group)], axis=0)
    tgt_pot = -tgt_half
    for it in range(ITERS):
        stand(tgt_pot)
        if it == 0:
            lax.fori_loop(near, held, forward, 0)
            settle(tall.at[0 : group - 1], first_recv.at[3])
            lax.fori_loop(0, held // 2, first_half, 0)
        else:
            lax.fori_loop(0, held, source_half, 0)
        xbuf[it, x] = close(s_top[...], s_sum[...])
        for d in far_first(nx):
            send(xbuf.at[it, x], xbuf.at[it, x], pair(it, 0), at_x(d))
        if nx > 1:
            settle(xbuf.at[it, 0 : nx - 1], iter_recv.at[it, 0])
        zbuf[it, z] = merge(xbuf[it])
        for d in far_first(nz):
            send(zbuf.at[it, z], zbuf.at[it, z], pair(it, 1), at_z(d))
        if it == 0:
            lax.fori_loop(0, held, build, 0)
        settle(zbuf.at[it, 0 : nz - 1], iter_recv.at[it, 1])
        src_pot = src_log - merge(zbuf[it])
        stand(src_pot)
        if it == ITERS - 1:
            for j in range(held):
                qrow[j] = src_pot[j : j + 1, :]

            @pl.when(shift == 0)
            def _():
                sib[0] = qrow[mine]
                send(sib.at[0], sib.at[1], sems(6), at_k(1))

        lax.fori_loop(0, blocks, target_half, 0)
        ybuf[it, seat] = close(t_top[...], t_sum[...])
        for d in range(1, group):
            send(ybuf.at[it, seat], ybuf.at[it, seat], pair(it, 2), at_seat(d))
        settle(ybuf.at[it, 0 : group - 1], iter_recv.at[it, 2])
        tgt_pot = tgt_log - merge(ybuf[it])

    result = (tgt_pot + tgt_half) * (1.0 / SCALE)
    for i in range(group):
        pots[i] = result[OWN * i : OWN * (i + 1), :]
    for yy in range(ny):
        obuf[z, yy] = pots[yy * nk + k]
    for d in far_first(nz):
        send(obuf.at[z], obuf.at[z], sems(7), at_z(d))

    @pl.when(shift == 0)
    def _():
        osrc_ref[...] = (sib[0] + src_half) * (1.0 / SCALE)
        settle(sib.at[0], first_send.at[6])
        settle(full.at[0 : nz - 1], first_send.at[0])
        settle(hold, first_send.at[2])

    @pl.when(shift != 0)
    def _():
        settle(sib.at[1], first_recv.at[6])
        osrc_ref[...] = (sib[1] + src_half) * (1.0 / SCALE)
        settle(own.at[0], first_send.at[1])

    settle(tall.at[0 : group - 1], first_send.at[3])
    settle(halves.at[0 : group - 1], first_send.at[8])
    settle(logs.at[:, 0], first_send.at[4])
    if nx > 1:
        settle(full.at[0 : held * (nx - 1)], first_send.at[5])
    for it in range(ITERS):
        if nx > 1:
            settle(xbuf.at[it, 0 : nx - 1], iter_send.at[it, 0])
        settle(zbuf.at[it, 0 : nz - 1], iter_send.at[it, 1])
        settle(ybuf.at[it, 0 : group - 1], iter_send.at[it, 2])
    settle(obuf.at[0 : nz - 1], first_recv.at[7])
    settle(obuf.at[0 : nz - 1], first_send.at[7])
    for zz in range(nz):
        for yy in range(ny):
            at = OWN * (yy * nz + zz)
            otgt_ref[at : at + OWN, :] = obuf[zz, yy]


def body(dims, *args):
    ny, nz, nx, nk = dims
    group = ny * nk
    held = nz // nk
    blocks = OWN * group
    f32, bf16 = jnp.float32, jnp.bfloat16
    dma = pltpu.SemaphoreType.DMA
    return pl.pallas_call(
        functools.partial(kernel, dims),
        out_shape=(
            jax.ShapeDtypeStruct((1, TILE), f32),
            jax.ShapeDtypeStruct((OWN * ny * nz, TILE), f32),
        ),
        in_specs=[pl.BlockSpec(memory_space=pl.ANY)] * 6,
        out_specs=(pl.BlockSpec(memory_space=pltpu.VMEM),) * 2,
        scratch_shapes=[
            pltpu.VMEM(args[0].shape, bf16),
            pltpu.VMEM(args[3].shape, f32),
            pltpu.VMEM(args[2].shape, f32),
            pltpu.SMEM(args[4].shape, jnp.int32),
            pltpu.SMEM(args[5].shape, jnp.int32),
            pltpu.VMEM((held * nx, TILE // nx, TILE), bf16),
            pltpu.VMEM((group, OWN * TILE, TILE), bf16),
            pltpu.VMEM((1, 1, 2 * TILE), f32),
            pltpu.VMEM((held, nk, 1, 2 * TILE), f32),
            pltpu.VMEM((nz - 1, nk, 1, 2 * TILE), f32),
            pltpu.VMEM((ny, nk, OWN, TILE), f32),
            pltpu.VMEM((group, OWN, TILE), f32),
            pltpu.VMEM((3 * held, held * TILE), bf16),
            pltpu.VMEM((3 * blocks, blocks * TILE), bf16),
            pltpu.VMEM((blocks, held, TILE), f32),
            pltpu.VMEM((held, blocks * TILE, TILE), f32),
            pltpu.VMEM((blocks, held * TILE, TILE), f32),
            pltpu.VMEM((max(held, blocks) * TILE, TILE), f32),
            pltpu.VMEM((held, blocks * 8, TILE), f32),
            pltpu.VMEM((held, blocks * 8, TILE), f32),
            pltpu.VMEM((blocks, held * 8, TILE), f32),
            pltpu.VMEM((blocks, held * 8, TILE), f32),
            pltpu.VMEM((ITERS, nx, held, TILE), f32),
            pltpu.VMEM((ITERS, nz, held, TILE), f32),
            pltpu.VMEM((ITERS, group, blocks, TILE), f32),
            pltpu.VMEM((held, 1, TILE), f32),
            pltpu.VMEM((2, 1, TILE), f32),
            pltpu.VMEM((group, OWN, TILE), f32),
            pltpu.VMEM((nz, ny, OWN, TILE), f32),
            dma((6,)),
            dma((2, held)),
            dma((9,)),
            dma((9,)),
            dma((ITERS, 3)),
            dma((ITERS, 3)),
        ],
        compiler_params=pltpu.CompilerParams(
            collective_id=0, has_side_effects=True, vmem_limit_bytes=56 * 2**20
        ),
    )(*args)


def solution(mesh, dims=(4, 16, 4, 2)):
    in_specs = (
        P("row", None),
        P(("col", "row"), None),
        P("row", None),
        P("col", None),
        P("row", "col", None, None),
        P("row", "col"),
    )
    out_specs = (P("row", None), P("col", None))
    return jax.shard_map(
        functools.partial(body, dims),
        mesh=mesh,
        in_specs=in_specs,
        out_specs=out_specs,
        check_vma=False,
    )
```

```python
import functools
import math

import jax
import jax.numpy as jnp
from jax import lax
from jax.experimental import pallas as pl
from jax.experimental.pallas import tpu as pltpu
from jax.sharding import PartitionSpec as P

ITERS = 3
EPSILON = 0.5
LOWEST = -1e30
SCALE = math.log2(math.e) / EPSILON
TILE = 128
OWN = 2
SHARE = 4

SRC_PARTS = 1
TGT_PARTS = 2
MESH = pl.DeviceIdType.MESH

def far_first(count):
    return sorted(range(1, count), key=lambda d: (-min(d, count - d), d))

def cross(left, right):
    return lax.dot_general(
        left, right, (((1,), (1,)), ((), ())), preferred_element_type=jnp.float32
    )

def half_norms(points):
    wide = points.astype(jnp.float32)
    square = wide * wide
    high = square.astype(jnp.bfloat16)
    low = (square - high.astype(jnp.float32)).astype(jnp.bfloat16)
    ones = jnp.ones((8, points.shape[1]), jnp.bfloat16)
    total = cross(ones, high) + cross(ones, low)
    return total[0:1] * (0.5 * SCALE)

def merge(parts):
    top = jnp.max(parts, axis=0)
    return top + jnp.log2(jnp.sum(jnp.exp2(parts - top[None]), axis=0))

def fold(s):
    s = s.reshape(s.shape[0] // 8, 8, TILE)
    top = jnp.max(s, axis=0)
    return top, jnp.sum(jnp.exp2(s - top[None]), axis=0)

def close(tops, sums):
    top = jnp.max(tops, axis=1)
    total = jnp.sum(jnp.exp2(tops - top[:, None, :]) * sums, axis=1)
    return top + jnp.log2(total)

def kernel(
    dims,
    src_hbm,
    tgt_hbm,
    smass_hbm,
    tmass_hbm,
    list_hbm,
    count_hbm,
    osrc_ref,
    otgt_ref,
    src,
    tmass,
    smass,
    slots,
    count,
    full,
    tall,
    own,
    meta,
    hold,
    logs,
    halves,
    picks_src,
    picks_tgt,
    bias,
    ts_score,
    st_score,
    columns,
    s_top,
    s_sum,
    t_top,
    t_sum,
    xbuf,
    zbuf,
    ybuf,
    qrow,
    sib,
    pots,
    obuf,
    local_sem,
    piece_sem,
    first_send,
    first_recv,
    iter_send,
    iter_recv,
):
    ny, nz, nx, nk = dims
    group = ny * nk
    held = nz // nk
    blocks = OWN * group
    part = TILE // nx
    row, col = lax.axis_index("row"), lax.axis_index("col")
    y, z = lax.div(row, nz), lax.rem(row, nz)
    x, k = lax.div(col, nk), lax.rem(col, nk)
    seat = y * nk + k
    mine = lax.div(z, nk)
    src_part, tgt_part = held // SRC_PARTS, blocks // TGT_PARTS
    src_share, tgt_share = min(SHARE, src_part), min(SHARE, tgt_part)
    shift = lax.rem(k + nz - lax.rem(z, nk), nk)

    def at_z(d):
        return (y * nz + lax.rem(z + d, nz), col)

    def at_x(d):
        return (row, lax.rem(x + d, nx) * nk + k)

    def at_k(d):
        return (row, x * nk + lax.rem(k + d, nk))

    def at_seat(d):
        other = lax.rem(seat + d, group)
        return (lax.div(other, nk) * nz + z, x * nk + lax.rem(other, nk))

    def send(src_ref, dst_ref, sems, where):
        pltpu.make_async_remote_copy(
            src_ref=src_ref,
            dst_ref=dst_ref,
            send_sem=sems[0],
            recv_sem=sems[1],
            device_id=where,
            device_id_type=MESH,
        ).start()

    def settle(ref, sem):
        pltpu.make_async_copy(ref, ref, sem).wait()

    loads = [
        pltpu.make_async_copy(src_hbm, src, local_sem.at[0]),
        pltpu.make_async_copy(tgt_hbm, tall.at[seat], local_sem.at[1]),
        pltpu.make_async_copy(smass_hbm, smass, local_sem.at[2]),
        pltpu.make_async_copy(tmass_hbm, tmass, local_sem.at[3]),
        pltpu.make_async_copy(list_hbm, slots, local_sem.at[4]),
        pltpu.make_async_copy(count_hbm, count, local_sem.at[5]),
    ]
    for load in loads:
        load.start()

    barrier = pltpu.get_barrier_semaphore()
    partners = (
        [at_z(d) for d in far_first(nz)]
        + [at_seat(d) for d in range(1, group)]
        + [at_x(d) for d in far_first(nx)]
    )
    for where in partners:
        pl.semaphore_signal(barrier, inc=1, device_id=where, device_id_type=MESH)
    for load in loads:
        load.wait()

    for picks in (picks_src, picks_tgt):
        n = picks.shape[0] // 3
        which = lax.rem(lax.broadcasted_iota(jnp.int32, picks.shape, 0), n)
        place = lax.div(lax.broadcasted_iota(jnp.int32, picks.shape, 1), TILE)
        picks[...] = jnp.where(which == place, 1.0, 0.0).astype(jnp.bfloat16)
    own_half = half_norms(tall[seat])
    for i in range(OWN):
        halves[seat, i : i + 1, :] = own_half[:, i * TILE : (i + 1) * TILE]
    src_half = half_norms(src[...])
    lane = lax.broadcasted_iota(jnp.int32, (1, TILE), 1)
    used = count[0, 0]
    live = jnp.zeros((1, TILE), jnp.float32)
    for slot in range(slots.shape[3]):
        block = jnp.where(slot < used, slots[0, 0, 1, slot], -1)
        live = jnp.where(lane == block, 1.0, live)
    own[0, :, 0:TILE] = jnp.where(live > 0.5, 0.0, LOWEST)
    own[0, :, TILE : 2 * TILE] = jnp.log2(smass[...])
    for yy in range(ny):
        at = OWN * nz * yy + OWN * z
        logs[yy, k] = jnp.log2(tmass[pl.ds(at, OWN), :])

    pl.semaphore_wait(barrier, len(partners))

    def sems(stage):
        return first_send.at[stage], first_recv.at[stage]

    my_slot = full.at[mine * nx + x]
    my_part = src.at[pl.ds(pl.multiple_of(x * part, part), part)]

    @pl.when(shift == 0)
    def _():
        for d in far_first(nz):
            send(my_part, my_slot, (first_send.at[0], piece_sem.at[0, mine]), at_z(d))
        pltpu.make_async_copy(my_part, my_slot, piece_sem.at[0, mine]).start()

    @pl.when(shift != 0)
    def _():
        send(own.at[0], meta.at[mine, k], sems(1), at_k(1))

    for d in range(1, group):
        send(halves.at[seat], halves.at[seat], sems(8), at_seat(d))
    for d in range(1, group):
        send(tall.at[seat], tall.at[seat], sems(3), at_seat(d))
    send(logs.at[:, k], logs.at[:, k], sems(4), at_k(1))

    @pl.when(shift == 0)
    def _():
        meta[mine, k] = own[0]
        settle(own.at[0], first_recv.at[1])
        for d in far_first(nz):
            send(meta.at[mine], meta.at[mine], sems(2), at_z(d))

    def slot_at(i):
        odd = lax.rem(i, 2)
        m = odd * lax.div(i + 1, 2) + (1 - odd) * lax.rem(held - lax.div(i, 2), held)
        return lax.div(lax.rem(z + shift + nk * m, nz), nk)

    def forward(i, carry):
        j = slot_at(i)
        settle(full.at[j * nx + x], piece_sem.at[0, j])
        for d in far_first(nx):
            piece = full.at[j * nx + x]
            send(piece, piece, (first_send.at[5], piece_sem.at[1, j]), at_x(d))
        return carry

    near = max(held - 3, 0)
    lax.fori_loop(0, near, forward, 0)

    @pl.when(shift == 0)
    def _():
        settle(meta.at[0 : held - 1], first_recv.at[2])

    @pl.when(shift != 0)
    def _():
        settle(meta, first_recv.at[2])

    for tb in range(blocks):
        drop = meta[:, tb // OWN % nk, 0, 0:TILE]
        at = OWN * nz * (tb // OWN // nk) + OWN * z + tb % OWN
        picked = jnp.sum(jnp.where(lane == at, drop, 0.0), axis=1, keepdims=True)
        bias[tb] = jnp.broadcast_to(picked, (held, TILE))
    src_log = meta[:, 0, 0, TILE : 2 * TILE]
    settle(logs.at[:, 0], first_recv.at[4])
    tgt_log = jnp.concatenate(
        [logs[i // nk, i % nk] for i in range(group)], axis=0
    )

    def stand(rows, at, picks):
        high = rows.astype(jnp.bfloat16).astype(jnp.float32)
        rest = rows - high
        middle = rest.astype(jnp.bfloat16).astype(jnp.float32)
        pieces = jnp.concatenate([high, middle, rest - middle], axis=0)
        turned = jnp.transpose(pieces).astype(jnp.bfloat16)
        spread = jnp.dot(turned, picks[...], preferred_element_type=jnp.float32)
        for b in range(rows.shape[0]):
            columns[(at + b) * TILE : (at + b + 1) * TILE, :] = spread[:, b * TILE : (b + 1) * TILE]

    def first_half(i, carry):
        pair_of = [slot_at(2 * i), slot_at(2 * i + 1)]
        if nx > 1:
            for j in pair_of:
                settle(full.at[pl.ds(j * nx, nx - 1)], piece_sem.at[1, j])
        source = jnp.concatenate(
            [full[pl.ds(j * nx, nx)].reshape(TILE, TILE) for j in pair_of], axis=0
        )
        for g in range(group):
            product = cross(tall[g], source) * SCALE
            for n in range(2 * OWN):
                u, v = n // 2, n % 2
                tb, j = OWN * g + u, pair_of[v]
                at = slice(tb * TILE, (tb + 1) * TILE)
                tile = product[u * TILE : (u + 1) * TILE, v * TILE : (v + 1) * TILE]
                tile = tile + bias[tb, pl.ds(j, 1), :]
                ts_score[j, at, :] = tile
                top, total = fold(tile + columns[at, :])
                s_top[j, tb * 8 : (tb + 1) * 8, :] = top
                s_sum[j, tb * 8 : (tb + 1) * 8, :] = total
        return carry

    def source_half(first, last):
        def run(step, carry):
            for tb in range(first, last):
                at = slice(tb * TILE, (tb + 1) * TILE)
                column = columns[at, :]
                for j in [src_share * step + n for n in range(src_share)]:
                    top, total = fold(ts_score[j, at, :] + column)
                    s_top[j, tb * 8 : (tb + 1) * 8, :] = top
                    s_sum[j, tb * 8 : (tb + 1) * 8, :] = total
            return carry

        return run

    def build(j, carry):
        source = full[pl.ds(j * nx, nx)].reshape(TILE, TILE)
        rows = pl.ds(pl.multiple_of(j * TILE, TILE), TILE)
        for g in range(group):
            product = cross(source, tall[g]) * SCALE
            for u in range(OWN):
                tb = OWN * g + u
                tile = product[:, u * TILE : (u + 1) * TILE]
                st_score[tb, rows, :] = tile + bias[tb, pl.ds(j, 1), :]
        return carry

    def target_half(first, last):
        def run(step, carry):
            for j in range(first, last):
                at = slice(j * TILE, (j + 1) * TILE)
                column = columns[at, :]
                for tb in [tgt_share * step + n for n in range(tgt_share)]:
                    top, total = fold(st_score[tb, at, :] + column)
                    t_top[tb, j * 8 : (j + 1) * 8, :] = top
                    t_sum[tb, j * 8 : (j + 1) * 8, :] = total
            return carry

        return run

    def pair(it, stage, p):
        return iter_send.at[it, stage, p], iter_recv.at[it, stage, p]

    def src_rows(p):
        return slice(p * src_part, (p + 1) * src_part)

    def tgt_rows(p):
        return slice(p * tgt_part, (p + 1) * tgt_part)

    def part_range(p, part, share):
        return p * part // share, (p + 1) * part // share

    def send_source(it, p):
        xbuf[it, p, x] = close(s_top[src_rows(p)], s_sum[src_rows(p)])
        for d in far_first(nx):
            send(xbuf.at[it, p, x], xbuf.at[it, p, x], pair(it, 0, p), at_x(d))

    def tgt_pot(it, p):
        settle(ybuf.at[it, p, 0 : group - 1], iter_recv.at[it, 2, p])
        return tgt_log[tgt_rows(p)] - merge(ybuf[it, p])

    settle(halves.at[0 : group - 1], first_recv.at[8])
    tgt_half = jnp.concatenate([halves[i] for i in range(group)], axis=0)
    for it in range(ITERS):
        if it == 0:
            for p in range(TGT_PARTS):
                stand(-tgt_half[tgt_rows(p)], p * tgt_part, picks_tgt)
            lax.fori_loop(near, held, forward, 0)
            settle(tall.at[0 : group - 1], first_recv.at[3])
            lax.fori_loop(0, held // 2, first_half, 0)
            for p in range(SRC_PARTS):
                send_source(it, p)
        else:
            for p in range(TGT_PARTS):
                stand(tgt_pot(it - 1, p), p * tgt_part, picks_tgt)
                if p < TGT_PARTS - 1:
                    run = source_half(p * tgt_part, (p + 1) * tgt_part)
                    lax.fori_loop(0, held // src_share, run, 0)
            for p in range(SRC_PARTS):
                run = source_half(blocks - tgt_part, blocks)
                lax.fori_loop(*part_range(p, src_part, src_share), run, 0)
                send_source(it, p)
        for p in range(SRC_PARTS):
            if nx > 1:
                settle(xbuf.at[it, p, 0 : nx - 1], iter_recv.at[it, 0, p])
            zbuf[it, p, z] = merge(xbuf[it, p])
            for d in far_first(nz):
                send(zbuf.at[it, p, z], zbuf.at[it, p, z], pair(it, 1, p), at_z(d))
        if it == 0:
            lax.fori_loop(0, held, build, 0)
        for p in range(SRC_PARTS):
            settle(zbuf.at[it, p, 0 : nz - 1], iter_recv.at[it, 1, p])
            src_pot = src_log[src_rows(p)] - merge(zbuf[it, p])
            stand(src_pot, p * src_part, picks_src)
            if it == ITERS - 1:
                for n in range(src_part):
                    qrow[p * src_part + n] = src_pot[n : n + 1, :]
            if p < SRC_PARTS - 1:
                run = target_half(p * src_part, (p + 1) * src_part)
                lax.fori_loop(0, blocks // tgt_share, run, 0)
        if it == ITERS - 1:

            @pl.when(shift == 0)
            def _():
                sib[0] = qrow[mine]
                send(sib.at[0], sib.at[1], sems(6), at_k(1))

        for p in range(TGT_PARTS):
            run = target_half(held - src_part, held)
            lax.fori_loop(*part_range(p, tgt_part, tgt_share), run, 0)
            ybuf[it, p, seat] = close(t_top[tgt_rows(p)], t_sum[tgt_rows(p)])
            for d in range(1, group):
                send(ybuf.at[it, p, seat], ybuf.at[it, p, seat], pair(it, 2, p), at_seat(d))

    last = jnp.concatenate([tgt_pot(ITERS - 1, p) for p in range(TGT_PARTS)], axis=0)
    result = (last + tgt_half) * (1.0 / SCALE)
    for i in range(group):
        pots[i] = result[OWN * i : OWN * (i + 1), :]
    for yy in range(ny):
        obuf[z, yy] = pots[yy * nk + k]
    for d in far_first(nz):
        send(obuf.at[z], obuf.at[z], sems(7), at_z(d))

    @pl.when(shift == 0)
    def _():
        osrc_ref[...] = (sib[0] + src_half) * (1.0 / SCALE)
        settle(sib.at[0], first_send.at[6])
        settle(full.at[0 : nz - 1], first_send.at[0])
        settle(hold, first_send.at[2])

    @pl.when(shift != 0)
    def _():
        settle(sib.at[1], first_recv.at[6])
        osrc_ref[...] = (sib[1] + src_half) * (1.0 / SCALE)
        settle(own.at[0], first_send.at[1])

    settle(tall.at[0 : group - 1], first_send.at[3])
    settle(halves.at[0 : group - 1], first_send.at[8])
    settle(logs.at[:, 0], first_send.at[4])
    if nx > 1:
        settle(full.at[0 : held * (nx - 1)], first_send.at[5])
    for it in range(ITERS):
        for p in range(SRC_PARTS):
            if nx > 1:
                settle(xbuf.at[it, p, 0 : nx - 1], iter_send.at[it, 0, p])
            settle(zbuf.at[it, p, 0 : nz - 1], iter_send.at[it, 1, p])
        for p in range(TGT_PARTS):
            settle(ybuf.at[it, p, 0 : group - 1], iter_send.at[it, 2, p])
    settle(obuf.at[0 : nz - 1], first_recv.at[7])
    settle(obuf.at[0 : nz - 1], first_send.at[7])
    for zz in range(nz):
        for yy in range(ny):
            at = OWN * (yy * nz + zz)
            otgt_ref[at : at + OWN, :] = obuf[zz, yy]

def body(dims, *args):
    ny, nz, nx, nk = dims
    group = ny * nk
    held = nz // nk
    blocks = OWN * group
    f32, bf16 = jnp.float32, jnp.bfloat16
    dma = pltpu.SemaphoreType.DMA
    return pl.pallas_call(
        functools.partial(kernel, dims),
        out_shape=(
            jax.ShapeDtypeStruct((1, TILE), f32),
            jax.ShapeDtypeStruct((OWN * ny * nz, TILE), f32),
        ),
        in_specs=[pl.BlockSpec(memory_space=pl.ANY)] * 6,
        out_specs=(pl.BlockSpec(memory_space=pltpu.VMEM),) * 2,
        scratch_shapes=[
            pltpu.VMEM(args[0].shape, bf16),
            pltpu.VMEM(args[3].shape, f32),
            pltpu.VMEM(args[2].shape, f32),
            pltpu.SMEM(args[4].shape, jnp.int32),
            pltpu.SMEM(args[5].shape, jnp.int32),
            pltpu.VMEM((held * nx, TILE // nx, TILE), bf16),
            pltpu.VMEM((group, OWN * TILE, TILE), bf16),
            pltpu.VMEM((1, 1, 2 * TILE), f32),
            pltpu.VMEM((held, nk, 1, 2 * TILE), f32),
            pltpu.VMEM((nz - 1, nk, 1, 2 * TILE), f32),
            pltpu.VMEM((ny, nk, OWN, TILE), f32),
            pltpu.VMEM((group, OWN, TILE), f32),
            pltpu.VMEM((3 * held // SRC_PARTS, held // SRC_PARTS * TILE), bf16),
            pltpu.VMEM((3 * blocks // TGT_PARTS, blocks // TGT_PARTS * TILE), bf16),
            pltpu.VMEM((blocks, held, TILE), f32),
            pltpu.VMEM((held, blocks * TILE, TILE), f32),
            pltpu.VMEM((blocks, held * TILE, TILE), f32),
            pltpu.VMEM((max(held, blocks) * TILE, TILE), f32),
            pltpu.VMEM((held, blocks * 8, TILE), f32),
            pltpu.VMEM((held, blocks * 8, TILE), f32),
            pltpu.VMEM((blocks, held * 8, TILE), f32),
            pltpu.VMEM((blocks, held * 8, TILE), f32),
            pltpu.VMEM((ITERS, SRC_PARTS, nx, held // SRC_PARTS, TILE), f32),
            pltpu.VMEM((ITERS, SRC_PARTS, nz, held // SRC_PARTS, TILE), f32),
            pltpu.VMEM((ITERS, TGT_PARTS, group, blocks // TGT_PARTS, TILE), f32),
            pltpu.VMEM((held, 1, TILE), f32),
            pltpu.VMEM((2, 1, TILE), f32),
            pltpu.VMEM((group, OWN, TILE), f32),
            pltpu.VMEM((nz, ny, OWN, TILE), f32),
            dma((6,)),
            dma((2, held)),
            dma((9,)),
            dma((9,)),
            dma((ITERS, 3, max(SRC_PARTS, TGT_PARTS))),
            dma((ITERS, 3, max(SRC_PARTS, TGT_PARTS))),
        ],
        compiler_params=pltpu.CompilerParams(
            collective_id=0, has_side_effects=True, vmem_limit_bytes=56 * 2**20
        ),
    )(*args)

def solution(mesh, dims=(4, 16, 4, 2)):
    in_specs = (
        P("row", None),
        P(("col", "row"), None),
        P("row", None),
        P("col", None),
        P("row", "col", None, None),
        P("row", "col"),
    )
    out_specs = (P("row", None), P("col", None))
    return jax.shard_map(
        functools.partial(body, dims),
        mesh=mesh,
        in_specs=in_specs,
        out_specs=out_specs,
        check_vma=False,
    )
```

```python
import functools
import math

import jax
import jax.numpy as jnp
from jax import lax
from jax.experimental import pallas as pl
from jax.experimental.pallas import tpu as pltpu
from jax.sharding import PartitionSpec as P

ITERS = 3
EPSILON = 0.5
LOWEST = -1e30
SCALE = math.log2(math.e) / EPSILON
TILE = 128
OWN = 2
SHARE = 4

SRC_PARTS = 1
TGT_PARTS = 2
MESH = pl.DeviceIdType.MESH

def far_first(count):
    return sorted(range(1, count), key=lambda d: (-min(d, count - d), d))

def cross(left, right):
    return lax.dot_general(
        left, right, (((1,), (1,)), ((), ())), preferred_element_type=jnp.float32
    )

def half_norms(points):
    wide = points.astype(jnp.float32)
    square = wide * wide
    high = square.astype(jnp.bfloat16)
    low = (square - high.astype(jnp.float32)).astype(jnp.bfloat16)
    ones = jnp.ones((8, points.shape[1]), jnp.bfloat16)
    total = cross(ones, high) + cross(ones, low)
    return total[0:1] * (0.5 * SCALE)

def merge(parts):
    top = jnp.max(parts, axis=0)
    return top + jnp.log2(jnp.sum(jnp.exp2(parts - top[None]), axis=0))

def fold(s):
    s = s.reshape(s.shape[0] // 8, 8, TILE)
    top = jnp.max(s, axis=0)
    return top, jnp.sum(jnp.exp2(s - top[None]), axis=0)

def close(tops, sums):
    top = jnp.max(tops, axis=1)
    total = jnp.sum(jnp.exp2(tops - top[:, None, :]) * sums, axis=1)
    return top + jnp.log2(total)

def kernel(
    dims,
    src_hbm,
    tgt_hbm,
    smass_hbm,
    tmass_hbm,
    list_hbm,
    count_hbm,
    osrc_ref,
    otgt_ref,
    src,
    tmass,
    smass,
    slots,
    count,
    full,
    tall,
    own,
    meta,
    hold,
    logs,
    halves,
    picks_src,
    picks_tgt,
    bias,
    ts_score,
    st_score,
    columns,
    s_top,
    s_sum,
    t_top,
    t_sum,
    xbuf,
    zbuf,
    ybuf,
    qrow,
    sib,
    pots,
    obuf,
    local_sem,
    piece_sem,
    first_send,
    first_recv,
    iter_send,
    iter_recv,
):
    ny, nz, nx, nk = dims
    group = ny * nk
    held = nz // nk
    blocks = OWN * group
    part = TILE // nx
    row, col = lax.axis_index("row"), lax.axis_index("col")
    y, z = lax.div(row, nz), lax.rem(row, nz)
    x, k = lax.div(col, nk), lax.rem(col, nk)
    seat = y * nk + k
    mine = lax.div(z, nk)
    src_part, tgt_part = held // SRC_PARTS, blocks // TGT_PARTS
    far_seats = sorted(range(1, group), key=lambda d: abs(d - group / 2))
    src_share, tgt_share = min(SHARE, src_part), min(SHARE, tgt_part)
    shift = lax.rem(k + nz - lax.rem(z, nk), nk)

    def at_z(d):
        return (y * nz + lax.rem(z + d, nz), col)

    def at_x(d):
        return (row, lax.rem(x + d, nx) * nk + k)

    def at_k(d):
        return (row, x * nk + lax.rem(k + d, nk))

    def at_seat(d):
        other = lax.rem(seat + d, group)
        return (lax.div(other, nk) * nz + z, x * nk + lax.rem(other, nk))

    def send(src_ref, dst_ref, sems, where):
        pltpu.make_async_remote_copy(
            src_ref=src_ref,
            dst_ref=dst_ref,
            send_sem=sems[0],
            recv_sem=sems[1],
            device_id=where,
            device_id_type=MESH,
        ).start()

    def settle(ref, sem):
        pltpu.make_async_copy(ref, ref, sem).wait()

    loads = [
        pltpu.make_async_copy(src_hbm, src, local_sem.at[0]),
        pltpu.make_async_copy(tgt_hbm, tall.at[seat], local_sem.at[1]),
        pltpu.make_async_copy(smass_hbm, smass, local_sem.at[2]),
        pltpu.make_async_copy(tmass_hbm, tmass, local_sem.at[3]),
        pltpu.make_async_copy(list_hbm, slots, local_sem.at[4]),
        pltpu.make_async_copy(count_hbm, count, local_sem.at[5]),
    ]
    for load in loads:
        load.start()

    barrier = pltpu.get_barrier_semaphore()
    partners = (
        [at_z(d) for d in far_first(nz)]
        + [at_seat(d) for d in range(1, group)]
        + [at_x(d) for d in far_first(nx)]
    )
    for where in partners:
        pl.semaphore_signal(barrier, inc=1, device_id=where, device_id_type=MESH)
    for load in loads:
        load.wait()

    for picks in (picks_src, picks_tgt):
        n = picks.shape[0] // 3
        which = lax.rem(lax.broadcasted_iota(jnp.int32, picks.shape, 0), n)
        place = lax.div(lax.broadcasted_iota(jnp.int32, picks.shape, 1), TILE)
        picks[...] = jnp.where(which == place, 1.0, 0.0).astype(jnp.bfloat16)
    own_half = half_norms(tall[seat])
    for i in range(OWN):
        halves[seat, i : i + 1, :] = own_half[:, i * TILE : (i + 1) * TILE]
    src_half = half_norms(src[...])
    lane = lax.broadcasted_iota(jnp.int32, (1, TILE), 1)
    used = count[0, 0]
    live = jnp.zeros((1, TILE), jnp.float32)
    for slot in range(slots.shape[3]):
        block = jnp.where(slot < used, slots[0, 0, 1, slot], -1)
        live = jnp.where(lane == block, 1.0, live)
    own[0, :, 0:TILE] = jnp.where(live > 0.5, 0.0, LOWEST)
    own[0, :, TILE : 2 * TILE] = jnp.log2(smass[...])
    for yy in range(ny):
        at = OWN * nz * yy + OWN * z
        logs[yy, k] = jnp.log2(tmass[pl.ds(at, OWN), :])

    pl.semaphore_wait(barrier, len(partners))

    def sems(stage):
        return first_send.at[stage], first_recv.at[stage]

    my_slot = full.at[mine * nx + x]
    my_part = src.at[pl.ds(pl.multiple_of(x * part, part), part)]

    @pl.when(shift == 0)
    def _():
        for d in far_first(nz):
            send(my_part, my_slot, (first_send.at[0], piece_sem.at[0, mine]), at_z(d))
        pltpu.make_async_copy(my_part, my_slot, piece_sem.at[0, mine]).start()

    @pl.when(shift != 0)
    def _():
        send(own.at[0], meta.at[mine, k], sems(1), at_k(1))

    for d in far_seats:
        send(halves.at[seat], halves.at[seat], sems(8), at_seat(d))
    for d in far_seats:
        send(tall.at[seat], tall.at[seat], sems(3), at_seat(d))
    send(logs.at[:, k], logs.at[:, k], sems(4), at_k(1))

    @pl.when(shift == 0)
    def _():
        meta[mine, k] = own[0]
        settle(own.at[0], first_recv.at[1])
        for d in far_first(nz):
            send(meta.at[mine], meta.at[mine], sems(2), at_z(d))

    def slot_at(i):
        odd = lax.rem(i, 2)
        m = odd * lax.div(i + 1, 2) + (1 - odd) * lax.rem(held - lax.div(i, 2), held)
        return lax.div(lax.rem(z + shift + nk * m, nz), nk)

    def forward(i, carry):
        j = slot_at(i)
        settle(full.at[j * nx + x], piece_sem.at[0, j])
        for d in far_first(nx):
            piece = full.at[j * nx + x]
            send(piece, piece, (first_send.at[5], piece_sem.at[1, j]), at_x(d))
        return carry

    near = max(held - 3, 0)
    lax.fori_loop(0, near, forward, 0)

    @pl.when(shift == 0)
    def _():
        settle(meta.at[0 : held - 1], first_recv.at[2])

    @pl.when(shift != 0)
    def _():
        settle(meta, first_recv.at[2])

    for tb in range(blocks):
        drop = meta[:, tb // OWN % nk, 0, 0:TILE]
        at = OWN * nz * (tb // OWN // nk) + OWN * z + tb % OWN
        picked = jnp.sum(jnp.where(lane == at, drop, 0.0), axis=1, keepdims=True)
        bias[tb] = jnp.broadcast_to(picked, (held, TILE))
    src_log = meta[:, 0, 0, TILE : 2 * TILE]
    settle(logs.at[:, 0], first_recv.at[4])
    tgt_log = jnp.concatenate(
        [logs[i // nk, i % nk] for i in range(group)], axis=0
    )

    def stand(rows, at, picks):
        high = rows.astype(jnp.bfloat16).astype(jnp.float32)
        rest = rows - high
        middle = rest.astype(jnp.bfloat16).astype(jnp.float32)
        pieces = jnp.concatenate([high, middle, rest - middle], axis=0)
        turned = jnp.transpose(pieces).astype(jnp.bfloat16)
        spread = jnp.dot(turned, picks[...], preferred_element_type=jnp.float32)
        for b in range(rows.shape[0]):
            columns[(at + b) * TILE : (at + b + 1) * TILE, :] = spread[:, b * TILE : (b + 1) * TILE]

    def first_half(i, carry):
        pair_of = [slot_at(2 * i), slot_at(2 * i + 1)]
        if nx > 1:
            for j in pair_of:
                settle(full.at[pl.ds(j * nx, nx - 1)], piece_sem.at[1, j])
        source = jnp.concatenate(
            [full[pl.ds(j * nx, nx)].reshape(TILE, TILE) for j in pair_of], axis=0
        )
        for g in range(group):
            product = cross(tall[g], source) * SCALE
            for n in range(2 * OWN):
                u, v = n // 2, n % 2
                tb, j = OWN * g + u, pair_of[v]
                at = slice(tb * TILE, (tb + 1) * TILE)
                tile = product[u * TILE : (u + 1) * TILE, v * TILE : (v + 1) * TILE]
                tile = tile + bias[tb, pl.ds(j, 1), :]
                ts_score[j, at, :] = tile
                top, total = fold(tile + columns[at, :])
                s_top[j, tb * 8 : (tb + 1) * 8, :] = top
                s_sum[j, tb * 8 : (tb + 1) * 8, :] = total
        return carry

    def source_half(first, last):
        def run(step, carry):
            for tb in range(first, last):
                at = slice(tb * TILE, (tb + 1) * TILE)
                column = columns[at, :]
                for j in [src_share * step + n for n in range(src_share)]:
                    top, total = fold(ts_score[j, at, :] + column)
                    s_top[j, tb * 8 : (tb + 1) * 8, :] = top
                    s_sum[j, tb * 8 : (tb + 1) * 8, :] = total
            return carry

        return run

    def build(j, carry):
        source = full[pl.ds(j * nx, nx)].reshape(TILE, TILE)
        rows = pl.ds(pl.multiple_of(j * TILE, TILE), TILE)
        for g in range(group):
            product = cross(source, tall[g]) * SCALE
            for u in range(OWN):
                tb = OWN * g + u
                tile = product[:, u * TILE : (u + 1) * TILE]
                st_score[tb, rows, :] = tile + bias[tb, pl.ds(j, 1), :]
        return carry

    def target_half(first, last):
        def run(step, carry):
            for j in range(first, last):
                at = slice(j * TILE, (j + 1) * TILE)
                column = columns[at, :]
                for tb in [tgt_share * step + n for n in range(tgt_share)]:
                    top, total = fold(st_score[tb, at, :] + column)
                    t_top[tb, j * 8 : (j + 1) * 8, :] = top
                    t_sum[tb, j * 8 : (j + 1) * 8, :] = total
            return carry

        return run

    def pair(it, stage, p):
        return iter_send.at[it, stage, p], iter_recv.at[it, stage, p]

    def src_rows(p):
        return slice(p * src_part, (p + 1) * src_part)

    def tgt_rows(p):
        return slice(p * tgt_part, (p + 1) * tgt_part)

    def part_range(p, part, share):
        return p * part // share, (p + 1) * part // share

    def send_source(it, p):
        xbuf[it, p, x] = close(s_top[src_rows(p)], s_sum[src_rows(p)])
        for d in far_first(nx):
            send(xbuf.at[it, p, x], xbuf.at[it, p, x], pair(it, 0, p), at_x(d))

    def tgt_pot(it, p):
        settle(ybuf.at[it, p, 0 : group - 1], iter_recv.at[it, 2, p])
        return tgt_log[tgt_rows(p)] - merge(ybuf[it, p])

    settle(halves.at[0 : group - 1], first_recv.at[8])
    tgt_half = jnp.concatenate([halves[i] for i in range(group)], axis=0)
    for it in range(ITERS):
        if it == 0:
            for p in range(TGT_PARTS):
                stand(-tgt_half[tgt_rows(p)], p * tgt_part, picks_tgt)
            lax.fori_loop(near, held, forward, 0)
            settle(tall.at[0 : group - 1], first_recv.at[3])
            lax.fori_loop(0, held // 2, first_half, 0)
            for p in range(SRC_PARTS):
                send_source(it, p)
        else:
            for p in range(TGT_PARTS):
                stand(tgt_pot(it - 1, p), p * tgt_part, picks_tgt)
                if p < TGT_PARTS - 1:
                    run = source_half(p * tgt_part, (p + 1) * tgt_part)
                    lax.fori_loop(0, held // src_share, run, 0)
            for p in range(SRC_PARTS):
                run = source_half(blocks - tgt_part, blocks)
                lax.fori_loop(*part_range(p, src_part, src_share), run, 0)
                send_source(it, p)
        for p in range(SRC_PARTS):
            if nx > 1:
                settle(xbuf.at[it, p, 0 : nx - 1], iter_recv.at[it, 0, p])
            zbuf[it, p, z] = merge(xbuf[it, p])
            for d in far_first(nz):
                send(zbuf.at[it, p, z], zbuf.at[it, p, z], pair(it, 1, p), at_z(d))
        if it == 0:
            lax.fori_loop(0, held, build, 0)
        for p in range(SRC_PARTS):
            settle(zbuf.at[it, p, 0 : nz - 1], iter_recv.at[it, 1, p])
            src_pot = src_log[src_rows(p)] - merge(zbuf[it, p])
            stand(src_pot, p * src_part, picks_src)
            if it == ITERS - 1:
                for n in range(src_part):
                    qrow[p * src_part + n] = src_pot[n : n + 1, :]
            if p < SRC_PARTS - 1:
                run = target_half(p * src_part, (p + 1) * src_part)
                lax.fori_loop(0, blocks // tgt_share, run, 0)
        if it == ITERS - 1:

            @pl.when(shift == 0)
            def _():
                sib[0] = qrow[mine]
                send(sib.at[0], sib.at[1], sems(6), at_k(1))

        for p in range(TGT_PARTS):
            run = target_half(held - src_part, held)
            lax.fori_loop(*part_range(p, tgt_part, tgt_share), run, 0)
            ybuf[it, p, seat] = close(t_top[tgt_rows(p)], t_sum[tgt_rows(p)])
            for d in far_seats:
                send(ybuf.at[it, p, seat], ybuf.at[it, p, seat], pair(it, 2, p), at_seat(d))

    last = jnp.concatenate([tgt_pot(ITERS - 1, p) for p in range(TGT_PARTS)], axis=0)
    result = (last + tgt_half) * (1.0 / SCALE)
    for i in range(group):
        pots[i] = result[OWN * i : OWN * (i + 1), :]
    for yy in range(ny):
        obuf[z, yy] = pots[yy * nk + k]
    for d in far_first(nz):
        send(obuf.at[z], obuf.at[z], sems(7), at_z(d))

    @pl.when(shift == 0)
    def _():
        osrc_ref[...] = (sib[0] + src_half) * (1.0 / SCALE)
        settle(sib.at[0], first_send.at[6])
        settle(full.at[0 : nz - 1], first_send.at[0])
        settle(hold, first_send.at[2])

    @pl.when(shift != 0)
    def _():
        settle(sib.at[1], first_recv.at[6])
        osrc_ref[...] = (sib[1] + src_half) * (1.0 / SCALE)
        settle(own.at[0], first_send.at[1])

    settle(tall.at[0 : group - 1], first_send.at[3])
    settle(halves.at[0 : group - 1], first_send.at[8])
    settle(logs.at[:, 0], first_send.at[4])
    if nx > 1:
        settle(full.at[0 : held * (nx - 1)], first_send.at[5])
    for it in range(ITERS):
        for p in range(SRC_PARTS):
            if nx > 1:
                settle(xbuf.at[it, p, 0 : nx - 1], iter_send.at[it, 0, p])
            settle(zbuf.at[it, p, 0 : nz - 1], iter_send.at[it, 1, p])
        for p in range(TGT_PARTS):
            settle(ybuf.at[it, p, 0 : group - 1], iter_send.at[it, 2, p])
    settle(obuf.at[0 : nz - 1], first_recv.at[7])
    settle(obuf.at[0 : nz - 1], first_send.at[7])
    for zz in range(nz):
        for yy in range(ny):
            at = OWN * (yy * nz + zz)
            otgt_ref[at : at + OWN, :] = obuf[zz, yy]

def body(dims, *args):
    ny, nz, nx, nk = dims
    group = ny * nk
    held = nz // nk
    blocks = OWN * group
    f32, bf16 = jnp.float32, jnp.bfloat16
    dma = pltpu.SemaphoreType.DMA
    return pl.pallas_call(
        functools.partial(kernel, dims),
        out_shape=(
            jax.ShapeDtypeStruct((1, TILE), f32),
            jax.ShapeDtypeStruct((OWN * ny * nz, TILE), f32),
        ),
        in_specs=[pl.BlockSpec(memory_space=pl.ANY)] * 6,
        out_specs=(pl.BlockSpec(memory_space=pltpu.VMEM),) * 2,
        scratch_shapes=[
            pltpu.VMEM(args[0].shape, bf16),
            pltpu.VMEM(args[3].shape, f32),
            pltpu.VMEM(args[2].shape, f32),
            pltpu.SMEM(args[4].shape, jnp.int32),
            pltpu.SMEM(args[5].shape, jnp.int32),
            pltpu.VMEM((held * nx, TILE // nx, TILE), bf16),
            pltpu.VMEM((group, OWN * TILE, TILE), bf16),
            pltpu.VMEM((1, 1, 2 * TILE), f32),
            pltpu.VMEM((held, nk, 1, 2 * TILE), f32),
            pltpu.VMEM((nz - 1, nk, 1, 2 * TILE), f32),
            pltpu.VMEM((ny, nk, OWN, TILE), f32),
            pltpu.VMEM((group, OWN, TILE), f32),
            pltpu.VMEM((3 * held // SRC_PARTS, held // SRC_PARTS * TILE), bf16),
            pltpu.VMEM((3 * blocks // TGT_PARTS, blocks // TGT_PARTS * TILE), bf16),
            pltpu.VMEM((blocks, held, TILE), f32),
            pltpu.VMEM((held, blocks * TILE, TILE), f32),
            pltpu.VMEM((blocks, held * TILE, TILE), f32),
            pltpu.VMEM((max(held, blocks) * TILE, TILE), f32),
            pltpu.VMEM((held, blocks * 8, TILE), f32),
            pltpu.VMEM((held, blocks * 8, TILE), f32),
            pltpu.VMEM((blocks, held * 8, TILE), f32),
            pltpu.VMEM((blocks, held * 8, TILE), f32),
            pltpu.VMEM((ITERS, SRC_PARTS, nx, held // SRC_PARTS, TILE), f32),
            pltpu.VMEM((ITERS, SRC_PARTS, nz, held // SRC_PARTS, TILE), f32),
            pltpu.VMEM((ITERS, TGT_PARTS, group, blocks // TGT_PARTS, TILE), f32),
            pltpu.VMEM((held, 1, TILE), f32),
            pltpu.VMEM((2, 1, TILE), f32),
            pltpu.VMEM((group, OWN, TILE), f32),
            pltpu.VMEM((nz, ny, OWN, TILE), f32),
            dma((6,)),
            dma((2, held)),
            dma((9,)),
            dma((9,)),
            dma((ITERS, 3, max(SRC_PARTS, TGT_PARTS))),
            dma((ITERS, 3, max(SRC_PARTS, TGT_PARTS))),
        ],
        compiler_params=pltpu.CompilerParams(
            collective_id=0, has_side_effects=True, vmem_limit_bytes=55104 * 1024
        ),
    )(*args)

def solution(mesh, dims=(4, 16, 4, 2)):
    in_specs = (
        P("row", None),
        P(("col", "row"), None),
        P("row", None),
        P("col", None),
        P("row", "col", None, None),
        P("row", "col"),
    )
    out_specs = (P("row", None), P("col", None))
    return jax.shard_map(
        functools.partial(body, dims),
        mesh=mesh,
        in_specs=in_specs,
        out_specs=out_specs,
        check_vma=False,
    )
```

```python
import functools
import math

import jax
import jax.numpy as jnp
from jax import lax
from jax.experimental import pallas as pl
from jax.experimental.pallas import tpu as pltpu
from jax.sharding import PartitionSpec as P

ITERS = 3
EPSILON = 0.5
LOWEST = -1e30
SCALE = math.log2(math.e) / EPSILON
TILE = 128
OWN = 2
SHARE = 4

SRC_PARTS = 1
TGT_PARTS = 2
MESH = pl.DeviceIdType.MESH

def far_first(count):
    return sorted(range(1, count), key=lambda d: (-min(d, count - d), d))

def cross(left, right):
    return lax.dot_general(
        left, right, (((1,), (1,)), ((), ())), preferred_element_type=jnp.float32
    )

def half_norms(points):
    wide = points.astype(jnp.float32)
    square = wide * wide
    high = square.astype(jnp.bfloat16)
    low = (square - high.astype(jnp.float32)).astype(jnp.bfloat16)
    ones = jnp.ones((8, points.shape[1]), jnp.bfloat16)
    total = cross(ones, high) + cross(ones, low)
    return total[0:1] * (0.5 * SCALE)

def merge(parts):
    top = jnp.max(parts, axis=0)
    return top + jnp.log2(jnp.sum(jnp.exp2(parts - top[None]), axis=0))

def fold(s):
    s = s.reshape(s.shape[0] // 8, 8, TILE)
    top = jnp.max(s, axis=0)
    return top, jnp.sum(jnp.exp2(s - top[None]), axis=0)

def close(tops, sums):
    top = jnp.max(tops, axis=1)
    total = jnp.sum(jnp.exp2(tops - top[:, None, :]) * sums, axis=1)
    return top + jnp.log2(total)

def kernel(
    dims,
    src_hbm,
    tgt_hbm,
    smass_hbm,
    tmass_hbm,
    list_hbm,
    count_hbm,
    osrc_ref,
    otgt_ref,
    src,
    tmass,
    smass,
    slots,
    count,
    full,
    tall,
    own,
    meta,
    hold,
    logs,
    halves,
    picks_src,
    picks_tgt,
    bias,
    ts_score,
    st_score,
    columns,
    s_top,
    s_sum,
    t_top,
    t_sum,
    xbuf,
    zbuf,
    ybuf,
    qrow,
    sib,
    pots,
    obuf,
    local_sem,
    piece_sem,
    first_send,
    first_recv,
    iter_send,
    iter_recv,
):
    ny, nz, nx, nk = dims
    group = ny * nk
    held = nz // nk
    blocks = OWN * group
    part = TILE // nx
    row, col = lax.axis_index("row"), lax.axis_index("col")
    y, z = lax.div(row, nz), lax.rem(row, nz)
    x, k = lax.div(col, nk), lax.rem(col, nk)
    seat = y * nk + k
    mine = lax.div(z, nk)
    src_part, tgt_part = held // SRC_PARTS, blocks // TGT_PARTS
    far_seats = sorted(range(1, group), key=lambda d: abs(d - group / 2))
    src_share, tgt_share = min(SHARE, src_part), min(SHARE, tgt_part)
    shift = lax.rem(k + nz - lax.rem(z, nk), nk)

    def at_z(d):
        return (y * nz + lax.rem(z + d, nz), col)

    def at_x(d):
        return (row, lax.rem(x + d, nx) * nk + k)

    def at_k(d):
        return (row, x * nk + lax.rem(k + d, nk))

    def at_seat(d):
        other = lax.rem(seat + d, group)
        return (lax.div(other, nk) * nz + z, x * nk + lax.rem(other, nk))

    def send(src_ref, dst_ref, sems, where):
        pltpu.make_async_remote_copy(
            src_ref=src_ref,
            dst_ref=dst_ref,
            send_sem=sems[0],
            recv_sem=sems[1],
            device_id=where,
            device_id_type=MESH,
        ).start()

    def settle(ref, sem):
        pltpu.make_async_copy(ref, ref, sem).wait()

    loads = [
        pltpu.make_async_copy(src_hbm, src, local_sem.at[0]),
        pltpu.make_async_copy(tgt_hbm, tall.at[seat], local_sem.at[1]),
        pltpu.make_async_copy(smass_hbm, smass, local_sem.at[2]),
        pltpu.make_async_copy(tmass_hbm, tmass, local_sem.at[3]),
        pltpu.make_async_copy(list_hbm, slots, local_sem.at[4]),
        pltpu.make_async_copy(count_hbm, count, local_sem.at[5]),
    ]
    for load in loads:
        load.start()

    barrier = pltpu.get_barrier_semaphore()
    partners = (
        [at_z(d) for d in far_first(nz)]
        + [at_seat(d) for d in range(1, group)]
        + [at_x(d) for d in far_first(nx)]
    )
    for where in partners:
        pl.semaphore_signal(barrier, inc=1, device_id=where, device_id_type=MESH)
    for load in loads:
        load.wait()

    for picks in (picks_src, picks_tgt):
        n = picks.shape[0] // 3
        which = lax.rem(lax.broadcasted_iota(jnp.int32, picks.shape, 0), n)
        place = lax.div(lax.broadcasted_iota(jnp.int32, picks.shape, 1), TILE)
        picks[...] = jnp.where(which == place, 1.0, 0.0).astype(jnp.bfloat16)
    own_half = half_norms(tall[seat])
    for i in range(OWN):
        halves[seat, i : i + 1, :] = own_half[:, i * TILE : (i + 1) * TILE]
    src_half = half_norms(src[...])
    lane = lax.broadcasted_iota(jnp.int32, (1, TILE), 1)
    used = count[0, 0]
    live = jnp.zeros((1, TILE), jnp.float32)
    for slot in range(slots.shape[3]):
        block = jnp.where(slot < used, slots[0, 0, 1, slot], -1)
        live = jnp.where(lane == block, 1.0, live)
    own[0, :, 0:TILE] = jnp.where(live > 0.5, 0.0, LOWEST)
    own[0, :, TILE : 2 * TILE] = jnp.log2(smass[...])
    for yy in range(ny):
        at = OWN * nz * yy + OWN * z
        logs[yy, k] = jnp.log2(tmass[pl.ds(at, OWN), :])

    pl.semaphore_wait(barrier, len(partners))

    def sems(stage):
        return first_send.at[stage], first_recv.at[stage]

    my_slot = full.at[mine * nx + x]
    my_part = src.at[pl.ds(pl.multiple_of(x * part, part), part)]

    @pl.when(shift == 0)
    def _():
        for d in far_first(nz):
            send(my_part, my_slot, (first_send.at[0], piece_sem.at[0, mine]), at_z(d))
        pltpu.make_async_copy(my_part, my_slot, piece_sem.at[0, mine]).start()

    @pl.when(shift != 0)
    def _():
        send(own.at[0], meta.at[mine, k], sems(1), at_k(1))

    for d in far_seats:
        send(halves.at[seat], halves.at[seat], sems(8), at_seat(d))
    for d in far_seats:
        send(tall.at[seat], tall.at[seat], sems(3), at_seat(d))
    send(logs.at[:, k], logs.at[:, k], sems(4), at_k(1))

    @pl.when(shift == 0)
    def _():
        meta[mine, k] = own[0]
        settle(own.at[0], first_recv.at[1])
        for d in far_first(nz):
            send(meta.at[mine], meta.at[mine], sems(2), at_z(d))

    def slot_at(i):
        odd = lax.rem(i, 2)
        m = odd * lax.div(i + 1, 2) + (1 - odd) * lax.rem(held - lax.div(i, 2), held)
        return lax.div(lax.rem(z + shift + nk * m, nz), nk)

    def forward(i, carry):
        j = slot_at(i)
        settle(full.at[j * nx + x], piece_sem.at[0, j])
        for d in far_first(nx):
            piece = full.at[j * nx + x]
            send(piece, piece, (first_send.at[5], piece_sem.at[1, j]), at_x(d))
        return carry

    near = max(held - 2, 0)
    lax.fori_loop(0, near, forward, 0)

    @pl.when(shift == 0)
    def _():
        settle(meta.at[0 : held - 1], first_recv.at[2])

    @pl.when(shift != 0)
    def _():
        settle(meta, first_recv.at[2])

    for tb in range(blocks):
        drop = meta[:, tb // OWN % nk, 0, 0:TILE]
        at = OWN * nz * (tb // OWN // nk) + OWN * z + tb % OWN
        picked = jnp.sum(jnp.where(lane == at, drop, 0.0), axis=1, keepdims=True)
        bias[tb] = jnp.broadcast_to(picked, (held, TILE))
    src_log = meta[:, 0, 0, TILE : 2 * TILE]
    settle(logs.at[:, 0], first_recv.at[4])
    tgt_log = jnp.concatenate(
        [logs[i // nk, i % nk] for i in range(group)], axis=0
    )

    def stand(rows, at, picks):
        high = rows.astype(jnp.bfloat16).astype(jnp.float32)
        rest = rows - high
        middle = rest.astype(jnp.bfloat16).astype(jnp.float32)
        pieces = jnp.concatenate([high, middle, rest - middle], axis=0)
        turned = jnp.transpose(pieces).astype(jnp.bfloat16)
        spread = jnp.dot(turned, picks[...], preferred_element_type=jnp.float32)
        for b in range(rows.shape[0]):
            columns[(at + b) * TILE : (at + b + 1) * TILE, :] = spread[:, b * TILE : (b + 1) * TILE]

    def first_half(i, carry):
        pair_of = [slot_at(2 * i), slot_at(2 * i + 1)]
        if nx > 1:
            for j in pair_of:
                settle(full.at[pl.ds(j * nx, nx - 1)], piece_sem.at[1, j])
        source = jnp.concatenate(
            [full[pl.ds(j * nx, nx)].reshape(TILE, TILE) for j in pair_of], axis=0
        )
        for g in range(group):
            product = cross(tall[g], source) * SCALE
            for n in range(2 * OWN):
                u, v = n // 2, n % 2
                tb, j = OWN * g + u, pair_of[v]
                at = slice(tb * TILE, (tb + 1) * TILE)
                tile = product[u * TILE : (u + 1) * TILE, v * TILE : (v + 1) * TILE]
                tile = tile + bias[tb, pl.ds(j, 1), :]
                ts_score[j, at, :] = tile
                top, total = fold(tile + columns[at, :])
                s_top[j, tb * 8 : (tb + 1) * 8, :] = top
                s_sum[j, tb * 8 : (tb + 1) * 8, :] = total
        return carry

    def source_half(first, last):
        def run(step, carry):
            for tb in range(first, last):
                at = slice(tb * TILE, (tb + 1) * TILE)
                column = columns[at, :]
                for j in [src_share * step + n for n in range(src_share)]:
                    top, total = fold(ts_score[j, at, :] + column)
                    s_top[j, tb * 8 : (tb + 1) * 8, :] = top
                    s_sum[j, tb * 8 : (tb + 1) * 8, :] = total
            return carry

        return run

    def build(j, carry):
        source = full[pl.ds(j * nx, nx)].reshape(TILE, TILE)
        rows = pl.ds(pl.multiple_of(j * TILE, TILE), TILE)
        for g in range(group):
            product = cross(source, tall[g]) * SCALE
            for u in range(OWN):
                tb = OWN * g + u
                tile = product[:, u * TILE : (u + 1) * TILE]
                st_score[tb, rows, :] = tile + bias[tb, pl.ds(j, 1), :]
        return carry

    def target_half(first, last):
        def run(step, carry):
            for j in range(first, last):
                at = slice(j * TILE, (j + 1) * TILE)
                column = columns[at, :]
                for tb in [tgt_share * step + n for n in range(tgt_share)]:
                    top, total = fold(st_score[tb, at, :] + column)
                    t_top[tb, j * 8 : (j + 1) * 8, :] = top
                    t_sum[tb, j * 8 : (j + 1) * 8, :] = total
            return carry

        return run

    def pair(it, stage, p):
        return iter_send.at[it, stage, p], iter_recv.at[it, stage, p]

    def src_rows(p):
        return slice(p * src_part, (p + 1) * src_part)

    def tgt_rows(p):
        return slice(p * tgt_part, (p + 1) * tgt_part)

    def part_range(p, part, share):
        return p * part // share, (p + 1) * part // share

    def send_source(it, p):
        xbuf[it, p, x] = close(s_top[src_rows(p)], s_sum[src_rows(p)])
        for d in far_first(nx):
            send(xbuf.at[it, p, x], xbuf.at[it, p, x], pair(it, 0, p), at_x(d))

    def tgt_pot(it, p):
        settle(ybuf.at[it, p, 0 : group - 1], iter_recv.at[it, 2, p])
        return tgt_log[tgt_rows(p)] - merge(ybuf[it, p])

    settle(halves.at[0 : group - 1], first_recv.at[8])
    tgt_half = jnp.concatenate([halves[i] for i in range(group)], axis=0)
    for it in range(ITERS):
        if it == 0:
            for p in range(TGT_PARTS):
                stand(-tgt_half[tgt_rows(p)], p * tgt_part, picks_tgt)
            lax.fori_loop(near, held, forward, 0)
            settle(tall.at[0 : group - 1], first_recv.at[3])
            lax.fori_loop(0, held // 2, first_half, 0)
            for p in range(SRC_PARTS):
                send_source(it, p)
        else:
            for p in range(TGT_PARTS):
                stand(tgt_pot(it - 1, p), p * tgt_part, picks_tgt)
                if p < TGT_PARTS - 1:
                    run = source_half(p * tgt_part, (p + 1) * tgt_part)
                    lax.fori_loop(0, held // src_share, run, 0)
            for p in range(SRC_PARTS):
                run = source_half(blocks - tgt_part, blocks)
                lax.fori_loop(*part_range(p, src_part, src_share), run, 0)
                send_source(it, p)
        for p in range(SRC_PARTS):
            if nx > 1:
                settle(xbuf.at[it, p, 0 : nx - 1], iter_recv.at[it, 0, p])
            zbuf[it, p, z] = merge(xbuf[it, p])
            for d in far_first(nz):
                send(zbuf.at[it, p, z], zbuf.at[it, p, z], pair(it, 1, p), at_z(d))
        if it == 0:
            lax.fori_loop(0, held, build, 0)
        for p in range(SRC_PARTS):
            settle(zbuf.at[it, p, 0 : nz - 1], iter_recv.at[it, 1, p])
            src_pot = src_log[src_rows(p)] - merge(zbuf[it, p])
            stand(src_pot, p * src_part, picks_src)
            if it == ITERS - 1:
                for n in range(src_part):
                    qrow[p * src_part + n] = src_pot[n : n + 1, :]
            if p < SRC_PARTS - 1:
                run = target_half(p * src_part, (p + 1) * src_part)
                lax.fori_loop(0, blocks // tgt_share, run, 0)
        if it == ITERS - 1:

            @pl.when(shift == 0)
            def _():
                sib[0] = qrow[mine]
                send(sib.at[0], sib.at[1], sems(6), at_k(1))

        for p in range(TGT_PARTS):
            run = target_half(held - src_part, held)
            lax.fori_loop(*part_range(p, tgt_part, tgt_share), run, 0)
            ybuf[it, p, seat] = close(t_top[tgt_rows(p)], t_sum[tgt_rows(p)])
            for d in far_seats:
                send(ybuf.at[it, p, seat], ybuf.at[it, p, seat], pair(it, 2, p), at_seat(d))

    last = jnp.concatenate([tgt_pot(ITERS - 1, p) for p in range(TGT_PARTS)], axis=0)
    result = (last + tgt_half) * (1.0 / SCALE)
    for i in range(group):
        pots[i] = result[OWN * i : OWN * (i + 1), :]
    for yy in range(ny):
        obuf[z, yy] = pots[yy * nk + k]
    for d in far_first(nz):
        send(obuf.at[z], obuf.at[z], sems(7), at_z(d))

    @pl.when(shift == 0)
    def _():
        osrc_ref[...] = (sib[0] + src_half) * (1.0 / SCALE)
        settle(sib.at[0], first_send.at[6])
        settle(full.at[0 : nz - 1], first_send.at[0])
        settle(hold, first_send.at[2])

    @pl.when(shift != 0)
    def _():
        settle(sib.at[1], first_recv.at[6])
        osrc_ref[...] = (sib[1] + src_half) * (1.0 / SCALE)
        settle(own.at[0], first_send.at[1])

    settle(tall.at[0 : group - 1], first_send.at[3])
    settle(halves.at[0 : group - 1], first_send.at[8])
    settle(logs.at[:, 0], first_send.at[4])
    if nx > 1:
        settle(full.at[0 : held * (nx - 1)], first_send.at[5])
    for it in range(ITERS):
        for p in range(SRC_PARTS):
            if nx > 1:
                settle(xbuf.at[it, p, 0 : nx - 1], iter_send.at[it, 0, p])
            settle(zbuf.at[it, p, 0 : nz - 1], iter_send.at[it, 1, p])
        for p in range(TGT_PARTS):
            settle(ybuf.at[it, p, 0 : group - 1], iter_send.at[it, 2, p])
    settle(obuf.at[0 : nz - 1], first_recv.at[7])
    settle(obuf.at[0 : nz - 1], first_send.at[7])
    for zz in range(nz):
        for yy in range(ny):
            at = OWN * (yy * nz + zz)
            otgt_ref[at : at + OWN, :] = obuf[zz, yy]

def body(dims, *args):
    ny, nz, nx, nk = dims
    group = ny * nk
    held = nz // nk
    blocks = OWN * group
    f32, bf16 = jnp.float32, jnp.bfloat16
    dma = pltpu.SemaphoreType.DMA
    return pl.pallas_call(
        functools.partial(kernel, dims),
        out_shape=(
            jax.ShapeDtypeStruct((1, TILE), f32),
            jax.ShapeDtypeStruct((OWN * ny * nz, TILE), f32),
        ),
        in_specs=[pl.BlockSpec(memory_space=pl.ANY)] * 6,
        out_specs=(pl.BlockSpec(memory_space=pltpu.VMEM),) * 2,
        scratch_shapes=[
            pltpu.VMEM(args[0].shape, bf16),
            pltpu.VMEM(args[3].shape, f32),
            pltpu.VMEM(args[2].shape, f32),
            pltpu.SMEM(args[4].shape, jnp.int32),
            pltpu.SMEM(args[5].shape, jnp.int32),
            pltpu.VMEM((held * nx, TILE // nx, TILE), bf16),
            pltpu.VMEM((group, OWN * TILE, TILE), bf16),
            pltpu.VMEM((1, 1, 2 * TILE), f32),
            pltpu.VMEM((held, nk, 1, 2 * TILE), f32),
            pltpu.VMEM((nz - 1, nk, 1, 2 * TILE), f32),
            pltpu.VMEM((ny, nk, OWN, TILE), f32),
            pltpu.VMEM((group, OWN, TILE), f32),
            pltpu.VMEM((3 * held // SRC_PARTS, held // SRC_PARTS * TILE), bf16),
            pltpu.VMEM((3 * blocks // TGT_PARTS, blocks // TGT_PARTS * TILE), bf16),
            pltpu.VMEM((blocks, held, TILE), f32),
            pltpu.VMEM((held, blocks * TILE, TILE), f32),
            pltpu.VMEM((blocks, held * TILE, TILE), f32),
            pltpu.VMEM((max(held, blocks) * TILE, TILE), f32),
            pltpu.VMEM((held, blocks * 8, TILE), f32),
            pltpu.VMEM((held, blocks * 8, TILE), f32),
            pltpu.VMEM((blocks, held * 8, TILE), f32),
            pltpu.VMEM((blocks, held * 8, TILE), f32),
            pltpu.VMEM((ITERS, SRC_PARTS, nx, held // SRC_PARTS, TILE), f32),
            pltpu.VMEM((ITERS, SRC_PARTS, nz, held // SRC_PARTS, TILE), f32),
            pltpu.VMEM((ITERS, TGT_PARTS, group, blocks // TGT_PARTS, TILE), f32),
            pltpu.VMEM((held, 1, TILE), f32),
            pltpu.VMEM((2, 1, TILE), f32),
            pltpu.VMEM((group, OWN, TILE), f32),
            pltpu.VMEM((nz, ny, OWN, TILE), f32),
            dma((6,)),
            dma((2, held)),
            dma((9,)),
            dma((9,)),
            dma((ITERS, 3, max(SRC_PARTS, TGT_PARTS))),
            dma((ITERS, 3, max(SRC_PARTS, TGT_PARTS))),
        ],
        compiler_params=pltpu.CompilerParams(
            collective_id=0, has_side_effects=True, vmem_limit_bytes=55104 * 1024
        ),
    )(*args)

def solution(mesh, dims=(4, 16, 4, 2)):
    in_specs = (
        P("row", None),
        P(("col", "row"), None),
        P("row", None),
        P("col", None),
        P("row", "col", None, None),
        P("row", "col"),
    )
    out_specs = (P("row", None), P("col", None))
    return jax.shard_map(
        functools.partial(body, dims),
        mesh=mesh,
        in_specs=in_specs,
        out_specs=out_specs,
        check_vma=False,
    )
```
